32 devices in a mesh: grp: 16 (over z, x, core), tp: 2 (over y).
Axes of the slice: x: 2, y: 2, z: 4, core: 2. Of those that a mesh axis runs over, the one named last changes fastest.
Arguments:
- prefill_states: bfloat16 [16384, 8192], P('grp', 'tp'), may hold values from -6 to 6
- key_weight: bfloat16 [8192, 1024], P('tp'), may hold values from -0.0625 to 0.0625
- value_weight: bfloat16 [8192, 1024], P('tp'), may hold values from -0.0625 to 0.0625
- offsets: int32 [16], P('grp'), may hold values from 0 to 7168, as said below
- matching: int32 [16], P('grp'), may hold values from 0 to 1, as said below
- queries: bfloat16 [512, 64, 128], P('grp', 'tp'), may hold values from -60 to 60
- cache_keys: bfloat16 [512, 8, 256, 128], P('grp', 'tp'), may hold values from -6 to 6
- cache_values: bfloat16 [512, 8, 256, 128], P('grp', 'tp'), may hold values from -6 to 6
- cache_lengths: int32 [512], P('grp'), may hold values from 1 to 256, as said below
Outputs:
- context: bfloat16 [512, 64, 128], P('grp', 'tp')
The draws below stay inside these ranges and needn't reach their ends.
Inputs may be any that keep to these rules, and one draw needn't show every extreme that they name: For each prompt p, the offsets of groups p * 8 to (p + 1) * 8 - 1 are 0, 1024, 2048, ... in some order, each once. `matching`: every prompt is continued by exactly 8 decode groups. `cache_lengths`: the first row of every group has 256 live entries.
All inputs are finite; a program needn't handle non-finite values.
Results may differ from the reference program's by a relative error of at most 0.012.
The reference program's roundings to bfloat16 on the way (of `page_keys`, `page_values` and `exponentials`) count: a program that leaves them out, or rounds other values in their place, can miss the bound.
Values may be sent and summed in bfloat16 or wider, within the bound.
No kernel may reach another device: no remote copies, remote signals or barrier semaphores. Data moves between devices by JAX's collectives and lax.ppermute only.
A program may use at most 320 MiB of HBM per device.

```python
import jax
import jax.numpy as jnp
from jax import lax

D = 8192
QH = 64
KVH = 8
HD = 128
BLOCK = 1024
ROWS = 32
GEN = 256
PROMPTS = 2
BLOCKS_PER_PROMPT = 8
PROMPT_LEN = 8192
PREFILL_TOKENS = 16384
DEC_ROWS = 512
N_GRP = 16


def shuffle(subkey):
    return jax.random.permutation(subkey, BLOCKS_PER_PROMPT)


def draw_offsets(key, part):
    key = jax.random.fold_in(key, 11)
    subkeys = jax.random.split(key, PROMPTS)
    orders = jax.vmap(shuffle)(subkeys)
    return (orders.reshape(-1) * BLOCK).astype(jnp.int32)


def draw_matching(key, part):
    key = jax.random.fold_in(key, 14)
    order = jax.random.permutation(key, N_GRP)
    return (order % PROMPTS).astype(jnp.int32)


def draw_queries(key, part):
    key = jax.random.fold_in(key, 12)
    return jnp.clip(jax.random.normal(key, (DEC_ROWS, QH, HD), jnp.float32), -6.0, 6.0).astype(jnp.bfloat16)


def draw_cache_lengths(key, part):
    key = jax.random.fold_in(key, 13)
    lengths = jax.random.randint(key, (DEC_ROWS,), 1, GEN + 1, jnp.int32)
    return lengths.at[::ROWS].set(GEN).astype(jnp.int32)


def levels(own_key, dims, pieces, least, largest):
    def one(dim, shards_of):
        heights = jax.random.uniform(jax.random.fold_in(jax.random.fold_in(own_key, 6), dim), (shards_of,), jnp.float32, least / len(pieces), largest / len(pieces))
        return jnp.repeat(jnp.exp(heights), dims[dim] // shards_of).reshape((-1,) + (1,) * (len(dims) - dim - 1))

    gain = one(*pieces[0])
    for cut in pieces[1:]:
        gain = gain * one(*cut)
    return gain


def noise(key, shape, width, most, shards=(), kind=jnp.bfloat16):
    gain = levels(key, shape, shards, -0.22, 0.18) if shards else 1.0
    values = jax.random.normal(key, shape, jnp.float32) * width * gain
    return jnp.minimum(jnp.maximum(values, -most), most).astype(kind)


def setup_inputs(seed: int = 0) -> dict:
    key_of = jax.random.split(jax.random.key(seed), 10)
    prefill_states = noise(key_of[0], (PREFILL_TOKENS, D), 1.0, 6.0, ((0, 16), (1, 2)))
    key_weight = noise(key_of[1], (D, KVH * HD), D ** -0.5, 0.0625, ((0, 2),))
    value_weight = noise(key_of[2], (D, KVH * HD), D ** -0.5, 0.0625, ((0, 2),))
    offsets = draw_offsets(jax.random.fold_in(key_of[9], 71), 0)
    matching = draw_matching(jax.random.fold_in(key_of[9], 71), 0)
    queries = draw_queries(jax.random.fold_in(key_of[9], 71), 0)
    cache_keys = noise(key_of[6], (DEC_ROWS, KVH, GEN, HD), 1.0, 6.0, ((0, 16), (1, 2)))
    cache_values = noise(key_of[7], (DEC_ROWS, KVH, GEN, HD), 1.0, 6.0, ((0, 16), (1, 2)))
    cache_lengths = draw_cache_lengths(jax.random.fold_in(key_of[9], 71), 0)
    return {"prefill_states": prefill_states, "key_weight": key_weight, "value_weight": value_weight, "offsets": offsets, "matching": matching, "queries": queries, "cache_keys": cache_keys, "cache_values": cache_values, "cache_lengths": cache_lengths}


def rotate(raw_heads, positions):
    half_width = HD // 2
    inverse_freq = 500000.0 ** (-(jnp.arange(half_width, dtype=jnp.float32) * 2.0 / HD))
    angles = positions.astype(jnp.float32)[:, None] * inverse_freq[None, :]
    cosine = jnp.cos(angles)[:, None, :]
    sine_part = jnp.sin(angles)[:, None, :]
    first_half = raw_heads[..., :half_width]
    second_half = raw_heads[..., half_width:]
    return jnp.concatenate([first_half * cosine - second_half * sine_part, second_half * cosine + first_half * sine_part], -1)


def reference(prefill_states, key_weight, value_weight, offsets, matching, queries, cache_keys, cache_values, cache_lengths):
    positions = (offsets[:, None] + jnp.arange(BLOCK, dtype=jnp.int32)[None, :]).reshape(-1)
    raw_keys = jnp.dot(prefill_states, key_weight, preferred_element_type=jnp.float32).reshape(-1, KVH, HD)
    page_keys = rotate(raw_keys, positions).astype(jnp.bfloat16)
    page_values = jnp.dot(prefill_states, value_weight, preferred_element_type=jnp.float32).astype(jnp.bfloat16).reshape(-1, KVH, HD)
    score_scale = HD ** -0.5

    def one_group(group):
        prompt_start = (matching[group] * PROMPT_LEN).astype(jnp.int32)
        prompt_keys = lax.dynamic_slice_in_dim(page_keys, prompt_start, PROMPT_LEN, 0).astype(jnp.float32)
        prompt_values = lax.dynamic_slice_in_dim(page_values, prompt_start, PROMPT_LEN, 0).astype(jnp.float32)
        row_start = (group * ROWS).astype(jnp.int32)
        query_rows = lax.dynamic_slice_in_dim(queries, row_start, ROWS, 0).astype(jnp.float32).reshape(ROWS, KVH, QH // KVH, HD)
        group_cache_keys = lax.dynamic_slice_in_dim(cache_keys, row_start, ROWS, 0).astype(jnp.float32)
        group_cache_values = lax.dynamic_slice_in_dim(cache_values, row_start, ROWS, 0).astype(jnp.float32)
        group_lengths = lax.dynamic_slice_in_dim(cache_lengths, row_start, ROWS, 0)
        prompt_scores = jnp.einsum('rkgd,lkd->rkgl', query_rows, prompt_keys) * score_scale
        cache_scores = jnp.einsum('rkgd,rktd->rkgt', query_rows, group_cache_keys) * score_scale
        alive_mask = (jnp.arange(GEN, dtype=jnp.int32)[None, :] < group_lengths[:, None])[:, None, None, :]
        cache_scores = jnp.where(alive_mask, cache_scores, -jnp.inf)
        all_scores = jnp.concatenate([prompt_scores, cache_scores], -1)
        row_top = all_scores.max(-1, keepdims=True)
        exponentials = jnp.exp(all_scores - row_top)
        total = exponentials.sum(-1)
        rounded = exponentials.astype(jnp.bfloat16).astype(jnp.float32)
        context = jnp.einsum('rkgl,lkd->rkgd', rounded[..., :PROMPT_LEN], prompt_values)
        context = context + jnp.einsum('rkgt,rktd->rkgd', rounded[..., PROMPT_LEN:], group_cache_values)
        context = context / total[..., None]
        return context.reshape(ROWS, QH, HD).astype(jnp.bfloat16)

    every_group = lax.map(one_group, jnp.arange(N_GRP, dtype=jnp.int32))
    return every_group.reshape(-1, QH, HD)
```

```python
import functools

import jax
import jax.numpy as jnp
import numpy as np
from jax import lax
from jax.experimental import pallas as pl
from jax.experimental.pallas import tpu as pltpu
from jax.sharding import PartitionSpec as P

HD = 128
PROMPTS = 2
CODE_BLOCKS = 16
CODE_TOP = 32000.0
STAT_ROWS = 16
EMPTY = -1e30
LOG2E = 1.4426950408889634
BIG = 60 * 1024 * 1024


def encode(values):
    rows = values.shape[0]
    blocks = values.reshape(CODE_BLOCKS, rows // CODE_BLOCKS, HD)
    largest = jnp.maximum(jnp.max(jnp.abs(blocks), axis=1), 1e-30)
    exponent = jnp.floor(jnp.log(largest) * LOG2E) + 1.0
    factor = jnp.exp2(-exponent) * CODE_TOP
    codes = jnp.round(blocks * factor[:, None, :]).astype(jnp.int32).astype(jnp.int16)
    return codes.reshape(rows, HD), exponent.astype(jnp.int32).astype(jnp.int16)


def decode(codes, exponent):
    rows = codes.shape[0]
    factor = jnp.exp2(exponent.astype(jnp.int32).astype(jnp.float32)) * (1.0 / CODE_TOP)
    blocks = codes.astype(jnp.int32).astype(jnp.float32).reshape(CODE_BLOCKS, rows // CODE_BLOCKS, HD)
    return (blocks * factor[:, None, :]).reshape(rows, HD)


def send_kernel(steps, heads, target_ref, x_ref, wk_ref, wv_ref, out_ref, key_acc, value_acc):
    step = pl.program_id(0)

    @pl.when(step == 0)
    def _():
        key_acc[...] = jnp.zeros_like(key_acc)
        value_acc[...] = jnp.zeros_like(value_acc)

    key_acc[...] += jnp.dot(x_ref[...], wk_ref[...], preferred_element_type=jnp.float32)
    value_acc[...] += jnp.dot(x_ref[...], wv_ref[...], preferred_element_type=jnp.float32)

    @pl.when(step == steps - 1)
    def _():
        rows = x_ref.shape[0]
        for head in range(heads):
            lanes = slice(head * HD, (head + 1) * HD)
            for half, acc in ((0, key_acc), (1, value_acc)):
                codes, exponent = encode(acc[:, lanes])
                out_ref[head, :rows, half * HD : (half + 1) * HD] = codes
                out_ref[head, rows:, half * HD : (half + 1) * HD] = exponent


def project_send(x, wk, wv, target, chunk, heads, kv_local):
    rows, depth = x.shape
    tile = min(512, depth)
    steps = depth // tile
    width = heads * HD
    per_target = kv_local // heads
    weight_spec = pl.BlockSpec((tile, width), lambda k, t: (k, t[0] * per_target + chunk))
    return pl.pallas_call(
        functools.partial(send_kernel, steps, heads),
        out_shape=jax.ShapeDtypeStruct((heads, rows + CODE_BLOCKS, 2 * HD), jnp.int16),
        grid_spec=pltpu.PrefetchScalarGridSpec(
            num_scalar_prefetch=1,
            grid=(steps,),
            in_specs=[pl.BlockSpec((rows, tile), lambda k, t: (0, k)), weight_spec, weight_spec],
            out_specs=pl.BlockSpec((heads, rows + CODE_BLOCKS, 2 * HD), lambda k, t: (0, 0, 0)),
            scratch_shapes=[pltpu.VMEM((rows, width), jnp.float32), pltpu.VMEM((rows, width), jnp.float32)],
        ),
        compiler_params=pltpu.CompilerParams(vmem_limit_bytes=BIG),
        cost_estimate=pl.CostEstimate(
            flops=4 * rows * depth * width,
            bytes_accessed=2 * rows * depth + 4 * depth * width + 4 * rows * width,
            transcendentals=0,
        ),
        name="project_send",
    )(target, x, wk, wv)


def own_kernel(target_ref, x_ref, wk_ref, wv_ref, key_ref, value_ref):
    @pl.when(pl.program_id(0) == 0)
    def _():
        key_ref[...] = jnp.zeros_like(key_ref)
        value_ref[...] = jnp.zeros_like(value_ref)

    key_ref[...] += jnp.dot(x_ref[...], wk_ref[...], preferred_element_type=jnp.float32)
    value_ref[...] += jnp.dot(x_ref[...], wv_ref[...], preferred_element_type=jnp.float32)


def project_own(x, wk, wv, target, kv_local):
    rows, depth = x.shape
    tile = min(512, depth)
    steps = depth // tile
    width = kv_local * HD
    weight_spec = pl.BlockSpec((tile, width), lambda k, t: (k, t[0]))
    out_spec = pl.BlockSpec((rows, width), lambda k, t: (0, 0))
    out_shape = jax.ShapeDtypeStruct((rows, width), jnp.float32)
    return pl.pallas_call(
        own_kernel,
        out_shape=(out_shape, out_shape),
        grid_spec=pltpu.PrefetchScalarGridSpec(
            num_scalar_prefetch=1,
            grid=(steps,),
            in_specs=[pl.BlockSpec((rows, tile), lambda k, t: (0, k)), weight_spec, weight_spec],
            out_specs=(out_spec, out_spec),
        ),
        compiler_params=pltpu.CompilerParams(vmem_limit_bytes=BIG),
        cost_estimate=pl.CostEstimate(
            flops=4 * rows * depth * width,
            bytes_accessed=2 * rows * depth + 4 * depth * width + 8 * rows * width,
            transcendentals=0,
        ),
        name="project_own",
    )(target, x, wk, wv)


def pack(context, logsum):
    high = logsum.astype(jnp.bfloat16).astype(jnp.float32)
    middle = (logsum - high).astype(jnp.bfloat16).astype(jnp.float32)
    low = logsum - high - middle
    line = lax.broadcasted_iota(jnp.int32, (STAT_ROWS, context.shape[1]), 0)
    stats = jnp.where(line == 0, high, jnp.where(line == 1, middle, jnp.where(line == 2, low, 0.0)))
    return context.astype(jnp.bfloat16), stats.astype(jnp.bfloat16)


def attend_kernel(
    parts, per, slots, order_ref, place_ref, key_ref, value_ref, cos_ref, sin_ref, q_ref, *rest
):
    received = rest[:parts]
    keep_ref, keep_log_ref, send_ref = rest[parts : parts + 3]
    key_scr, value_scr, context_scr, log_scr = rest[parts + 3 :]
    rows = key_ref.shape[0]
    keys = key_ref[...]
    values = value_ref[...]
    for part in received:
        keys = keys + decode(part[0, :rows, :HD], part[0, rows:, :HD])
        values = values + decode(part[0, :rows, HD:], part[0, rows:, HD:])
    keys = keys * cos_ref[...] + pltpu.roll(keys, HD // 2, 1) * sin_ref[...]
    key_scr[...] = keys.astype(jnp.bfloat16)
    value_scr[...] = jnp.transpose(values).astype(jnp.bfloat16)
    to_log2 = HD ** (-0.5) * LOG2E

    def one(index):
        scores = jnp.dot(key_scr[...], q_ref[order_ref[index]], preferred_element_type=jnp.float32)
        top = jnp.max(scores, axis=0, keepdims=True) * to_log2
        weights = jnp.exp2(scores * to_log2 - top)
        total = jnp.sum(weights, axis=0, keepdims=True)
        summed = jnp.dot(value_scr[...], weights.astype(jnp.bfloat16), preferred_element_type=jnp.float32)
        context_scr[place_ref[index]] = summed * (1.0 / total)
        log_scr[place_ref[index]] = jnp.broadcast_to(top + jnp.log(total) * LOG2E, log_scr.shape[1:])

    def empty(index):
        context_scr[place_ref[index]] = jnp.zeros(context_scr.shape[1:], jnp.float32)
        log_scr[place_ref[index]] = jnp.full(log_scr.shape[1:], EMPTY, jnp.float32)

    @pl.loop(0, per // 2)
    def _(index):
        one(2 * index)
        one(2 * index + 1)

    @pl.loop(per, slots)
    def _(index):
        empty(index)

    half = slots // 2
    for slot in range(half):
        keep_ref[0, slot] = context_scr[slot]
        keep_log_ref[0, slot] = log_scr[slot]
        context, stats = pack(context_scr[half + slot], log_scr[half + slot][:1])
        send_ref[0, slot, :HD] = context
        send_ref[0, slot, HD:] = stats


def attend(order, place, keys, values, cosine, sine, q_all, received, chunk, heads, per):
    rows = keys.shape[0]
    slots, _, wide = q_all.shape
    half = slots // 2
    head_spec = pl.BlockSpec((rows, HD), lambda h, a, b: (0, chunk * heads + h))
    table_spec = pl.BlockSpec((rows, HD), lambda h, a, b: (0, 0))
    part_spec = pl.BlockSpec((1, rows + CODE_BLOCKS, 2 * HD), lambda h, a, b: (h, 0, 0))

    def slot_spec(depth):
        return pl.BlockSpec((1, half, depth, wide), lambda h, a, b: (h, 0, 0, 0))

    return pl.pallas_call(
        functools.partial(attend_kernel, len(received), per, slots),
        out_shape=(
            jax.ShapeDtypeStruct((heads, half, HD, wide), jnp.float32),
            jax.ShapeDtypeStruct((heads, half, 8, wide), jnp.float32),
            jax.ShapeDtypeStruct((heads, half, HD + STAT_ROWS, wide), jnp.bfloat16),
        ),
        grid_spec=pltpu.PrefetchScalarGridSpec(
            num_scalar_prefetch=2,
            grid=(heads,),
            in_specs=[
                head_spec,
                head_spec,
                table_spec,
                table_spec,
                pl.BlockSpec((slots, HD, wide), lambda h, a, b: (0, chunk * heads + h, 0)),
            ]
            + [part_spec] * len(received),
            out_specs=(slot_spec(HD), slot_spec(8), slot_spec(HD + STAT_ROWS)),
            scratch_shapes=[
                pltpu.VMEM((rows, HD), jnp.bfloat16),
                pltpu.VMEM((HD, rows), jnp.bfloat16),
                pltpu.VMEM((slots, HD, wide), jnp.float32),
                pltpu.VMEM((slots, 8, wide), jnp.float32),
            ],
        ),
        compiler_params=pltpu.CompilerParams(vmem_limit_bytes=BIG),
        cost_estimate=pl.CostEstimate(
            flops=8 * heads * per * rows * wide * HD,
            bytes_accessed=heads * (rows * HD * 16 + slots * HD * wide * 6),
            transcendentals=heads * per * rows * wide,
        ),
        name="attend",
    )(order, place, keys, values, cosine, sine, q_all, *received)


def merge_kernel(last, keep_ref, keep_log_ref, part_ref, *outs):
    heads, count = keep_ref.shape[:2]
    half = count // 2
    for head in range(heads):
        for slot in range(count):
            stats = part_ref[head, slot, HD:].astype(jnp.float32)
            other_log = stats[0:1] + stats[1:2] + stats[2:3]
            own_log = keep_log_ref[head, slot][:1]
            top = jnp.maximum(own_log, other_log)
            own_share = jnp.exp2(own_log - top)
            other_share = jnp.exp2(other_log - top)
            total = own_share + other_share
            inverse = 1.0 / total
            context = keep_ref[head, slot] * (own_share * inverse) + part_ref[
                head, slot, :HD
            ].astype(jnp.float32) * (other_share * inverse)
            logsum = top + jnp.log(total) * LOG2E
            if last:
                outs[0][head] = jnp.transpose(context)
                outs[1][head] = jnp.broadcast_to(logsum, (8, logsum.shape[1]))
            elif slot < half:
                outs[0][head, slot] = context
                outs[1][head, slot] = jnp.broadcast_to(logsum, (8, logsum.shape[1]))
            else:
                packed, stats = pack(context, logsum)
                outs[2][head, slot - half, :HD] = packed
                outs[2][head, slot - half, HD:] = stats


def merge(keep, keep_log, part):
    heads, count, _, wide = keep.shape
    half = count // 2
    last = count == 1
    if last:
        out_shape = (
            jax.ShapeDtypeStruct((heads, wide, HD), jnp.float32),
            jax.ShapeDtypeStruct((heads, 8, wide), jnp.float32),
        )
    else:
        out_shape = (
            jax.ShapeDtypeStruct((heads, half, HD, wide), jnp.float32),
            jax.ShapeDtypeStruct((heads, half, 8, wide), jnp.float32),
            jax.ShapeDtypeStruct((heads, half, HD + STAT_ROWS, wide), jnp.bfloat16),
        )
    return pl.pallas_call(
        functools.partial(merge_kernel, last),
        out_shape=out_shape,
        compiler_params=pltpu.CompilerParams(vmem_limit_bytes=BIG),
        cost_estimate=pl.CostEstimate(
            flops=4 * heads * count * HD * wide,
            bytes_accessed=heads * count * HD * wide * 9,
            transcendentals=0,
        ),
        name="merge",
    )(keep, keep_log, part)


def tables(offset, rows):
    half_width = HD // 2
    inverse_freq = 500000.0 ** (-(jnp.arange(half_width, dtype=jnp.float32) * 2.0 / HD))
    positions = offset + jnp.arange(rows, dtype=jnp.int32)
    angles = positions.astype(jnp.float32)[:, None] * inverse_freq[None, :]
    cosine = jnp.cos(angles)
    sine = jnp.sin(angles)
    return jnp.concatenate([cosine, cosine], 1), jnp.concatenate([-sine, sine], 1)


def bit_reversed(values, bits):
    flipped = jnp.zeros_like(values)
    for bit in range(bits):
        flipped = flipped + (((values >> bit) & 1) << (bits - 1 - bit))
    return flipped


def on_device(
    prefill_states,
    key_weight,
    value_weight,
    offsets,
    matching,
    queries,
    cache_keys,
    cache_values,
    cache_lengths,
):
    tp = lax.axis_size("tp")
    groups = lax.axis_size("grp")
    per = groups // PROMPTS
    bits = groups.bit_length() - 1
    me = lax.axis_index("grp")
    rank = lax.axis_index("tp")
    block_len = prefill_states.shape[0]
    kv_local = key_weight.shape[1] // HD // tp
    row_count = queries.shape[0]
    group_size = queries.shape[1] // kv_local
    wide = row_count * group_size
    heads = 2 if kv_local % 2 == 0 else 1
    chunks = kv_local // heads

    grouped = queries.reshape(row_count, kv_local, group_size, HD)
    turned = grouped.transpose(1, 3, 0, 2).reshape(kv_local * HD, wide)
    tag = jnp.broadcast_to(matching[0].astype(jnp.bfloat16), (STAT_ROWS, wide))
    q_all = lax.all_gather(jnp.concatenate([turned, tag], 0), "grp")
    wanted = q_all[:, kv_local * HD, 0].astype(jnp.int32)

    received = []
    for chunk in range(chunks):
        parts = []
        for shift in range(1, tp):
            target = ((rank + shift) % tp).astype(jnp.int32).reshape(1)
            coded = project_send(
                prefill_states, key_weight, value_weight, target, chunk, heads, kv_local
            )
            parts.append(
                lax.ppermute(coded, "tp", [(i, (i + shift) % tp) for i in range(tp)])
            )
        received.append(parts)
    own_keys, own_values = project_own(
        prefill_states, key_weight, value_weight, rank.astype(jnp.int32).reshape(1), kv_local
    )
    cosine, sine = tables(offsets[0], block_len)

    mine = (wanted == me // per).astype(jnp.int32)
    rank_in = jnp.cumsum(mine) - 1
    rank_out = per + jnp.cumsum(1 - mine) - 1
    spot = jnp.where(mine == 1, rank_in, rank_out)
    names = jnp.arange(groups, dtype=jnp.int32)
    order = jnp.sum(jnp.where(spot[None, :] == names[:, None], names[None, :], 0), 1).astype(jnp.int32)
    place = bit_reversed(order ^ me.astype(jnp.int32), bits)

    score_scale = HD ** (-0.5)
    cache_len = cache_keys.shape[2]
    cache_scores = (
        jnp.einsum("rkgd,rktd->rkgt", grouped, cache_keys, preferred_element_type=jnp.float32)
        * score_scale
    )
    alive = (jnp.arange(cache_len, dtype=jnp.int32)[None, :] < cache_lengths[:, None])[:, None, None, :]
    cache_scores = jnp.where(alive, cache_scores, EMPTY)
    cache_top = cache_scores.max(-1)
    cache_weights = jnp.where(alive, jnp.exp(cache_scores - cache_top[..., None]), 0.0)
    cache_total = cache_weights.sum(-1)
    cache_sum = jnp.einsum(
        "rkgt,rktd->rkgd",
        cache_weights.astype(jnp.bfloat16),
        cache_values,
        preferred_element_type=jnp.float32,
    )

    contexts = []
    logs = []
    for chunk in range(chunks):
        keep, keep_log, send = attend(
            order, place, own_keys, own_values, cosine, sine, q_all, received[chunk], chunk, heads, per
        )
        for bit in range(bits):
            arrived = lax.ppermute(send, "grp", [(i, i ^ (1 << bit)) for i in range(groups)])
            if bit < bits - 1:
                keep, keep_log, send = merge(keep, keep_log, arrived)
            else:
                context, log = merge(keep, keep_log, arrived)
        contexts.append(context)
        logs.append(log[:, 0])
    prompt_context = jnp.concatenate(contexts, 0).reshape(kv_local, row_count, group_size, HD)
    prompt_context = prompt_context.transpose(1, 0, 2, 3)
    prompt_log = jnp.concatenate(logs, 0).reshape(kv_local, row_count, group_size).transpose(1, 0, 2)
    cache_log = cache_top * LOG2E
    top = jnp.maximum(prompt_log, cache_log)
    prompt_share = jnp.exp2(prompt_log - top)
    cache_share = jnp.exp2(cache_log - top)
    total = prompt_share + cache_share * cache_total
    context = (prompt_context * prompt_share[..., None] + cache_sum * cache_share[..., None]) / total[..., None]
    return context.reshape(row_count, kv_local * group_size, HD).astype(jnp.bfloat16)


def solution(mesh):
    placed = (
        P("grp", "tp"),
        P("tp", None),
        P("tp", None),
        P("grp"),
        P("grp"),
        P("grp", "tp", None),
        P("grp", "tp", None, None),
        P("grp", "tp", None, None),
        P("grp"),
    )
    return jax.shard_map(
        on_device, mesh=mesh, in_specs=placed, out_specs=P("grp", "tp", None), check_vma=False
    )
```

```python
import functools

import jax
import jax.numpy as jnp
from jax import lax
from jax.experimental import pallas as pl
from jax.experimental.pallas import tpu as pltpu
from jax.sharding import PartitionSpec as P

HD = 128
PROMPTS = 2
CODE_BLOCKS = 16
CODE_TOP = 32000.0
STAT_ROWS = 16
EMPTY = -1e30
LOG2E = 1.4426950408889634
TO_LOG2 = HD ** (-0.5) * LOG2E
BIG = 60 * 1024 * 1024
ANY = pl.BlockSpec(memory_space=pl.ANY)


def encode(values):
    rows = values.shape[0]
    blocks = values.reshape(CODE_BLOCKS, rows // CODE_BLOCKS, HD)
    largest = jnp.maximum(jnp.max(jnp.abs(blocks), axis=1), 1e-30)
    exponent = jnp.floor(jnp.log(largest) * LOG2E) + 1.0
    factor = jnp.exp2(-exponent) * CODE_TOP
    codes = jnp.round(blocks * factor[:, None, :]).astype(jnp.int32).astype(jnp.int16)
    return codes.reshape(rows, HD), exponent.astype(jnp.int32).astype(jnp.int16)


def decode(codes, exponent):
    rows = codes.shape[0]
    factor = jnp.exp2(exponent.astype(jnp.int32).astype(jnp.float32)) * (1.0 / CODE_TOP)
    blocks = codes.astype(jnp.int32).astype(jnp.float32).reshape(CODE_BLOCKS, rows // CODE_BLOCKS, HD)
    return (blocks * factor[:, None, :]).reshape(rows, HD)


def project_kernel(plan, split, pieces, place_ref, x_hbm, wk_ref, wv_ref, *rest):
    count = sum(split - (kind == "own") for kind in plan) + 2 * plan.count("own")
    outs = rest[:count]
    x_ref, acc, sems = rest[count:]
    step = pl.program_id(0)
    rows = x_ref.shape[0]
    width = wk_ref.shape[1]
    part = rows // pieces

    def fetch(piece):
        window = pl.ds(piece * part, part)
        return pltpu.make_async_copy(x_hbm.at[window], x_ref.at[window], sems.at[piece])

    @pl.when(step == 0)
    def _():
        for piece in range(pieces):
            fetch(piece).start()

    for piece in range(pieces):

        @pl.when(step == 0)
        def _():
            fetch(piece).wait()

        window = pl.ds(piece * part, part)
        acc[window, :width] = jnp.dot(x_ref[window], wk_ref[...], preferred_element_type=jnp.float32)
        acc[window, width:] = jnp.dot(x_ref[window], wv_ref[...], preferred_element_type=jnp.float32)

    core = place_ref[0]
    index = 0
    for number, kind in enumerate(plan):
        here = list(outs[index : index + split + (kind == "own")])
        index += split + (kind == "own")

        @pl.when(step == number)
        def _():
            refs = list(here)
            for apart in range(split):
                lanes = pl.multiple_of((core ^ apart) * HD, HD)
                if kind == "own" and apart == 0:
                    refs.pop(0)[...] = acc[:, pl.ds(lanes, HD)]
                    refs.pop(0)[...] = acc[:, pl.ds(width + lanes, HD)]
                    continue
                ref = refs.pop(0)
                for half in range(2):
                    codes, exponent = encode(acc[:, pl.ds(half * width + lanes, HD)])
                    ref[:rows, half * HD : (half + 1) * HD] = codes
                    ref[rows:, half * HD : (half + 1) * HD] = exponent


def project(x, wk, wv, core, columns, plan, split):
    rows, depth = x.shape
    width = split * HD
    steps = len(plan)
    pieces = 2
    coded = jax.ShapeDtypeStruct((rows + CODE_BLOCKS, 2 * HD), jnp.int16)
    plain = jax.ShapeDtypeStruct((rows, HD), jnp.float32)
    shapes = []
    for kind in plan:
        shapes += ([plain, plain] if kind == "own" else [coded]) + [coded] * (split - 1)
    weight_spec = pl.BlockSpec((depth, width), lambda s, p: (0, p[1 + s]))
    place = jnp.stack([core] + columns).astype(jnp.int32)
    outs = pl.pallas_call(
        functools.partial(project_kernel, plan, split, pieces),
        out_shape=tuple(shapes),
        grid_spec=pltpu.PrefetchScalarGridSpec(
            num_scalar_prefetch=1,
            grid=(steps,),
            in_specs=[ANY, weight_spec, weight_spec],
            out_specs=tuple(pl.BlockSpec(shape.shape, lambda s, p: (0, 0)) for shape in shapes),
            scratch_shapes=[
                pltpu.VMEM((rows, depth), x.dtype),
                pltpu.VMEM((rows, 2 * width), jnp.float32),
                pltpu.SemaphoreType.DMA((pieces,)),
            ],
        ),
        compiler_params=pltpu.CompilerParams(vmem_limit_bytes=BIG),
        cost_estimate=pl.CostEstimate(
            flops=4 * rows * depth * width * steps,
            bytes_accessed=2 * rows * depth + steps * (4 * depth * width + 4 * rows * width),
            transcendentals=0,
        ),
        name="project",
    )(place, x, wk, wv)
    results = []
    index = 0
    for kind in plan:
        size = split + (kind == "own")
        results.append(list(outs[index : index + size]))
        index += size
    return results


def pack(context, logsum):
    high = logsum.astype(jnp.bfloat16).astype(jnp.float32)
    middle = (logsum - high).astype(jnp.bfloat16).astype(jnp.float32)
    low = logsum - high - middle
    line = lax.broadcasted_iota(jnp.int32, (STAT_ROWS, context.shape[1]), 0)
    stats = jnp.where(line == 0, high, jnp.where(line == 1, middle, jnp.where(line == 2, low, 0.0)))
    return context.astype(jnp.bfloat16), stats.astype(jnp.bfloat16)


def unpack(block):
    stats = block[HD:].astype(jnp.float32)
    return block[:HD].astype(jnp.float32), stats[0:1] + stats[1:2] + stats[2:3]


def blend(pieces):
    top = functools.reduce(jnp.maximum, [logsum for _, logsum in pieces])
    shares = [jnp.exp2(logsum - top) for _, logsum in pieces]
    total = functools.reduce(jnp.add, shares)
    inverse = 1.0 / total
    context = functools.reduce(
        jnp.add, [context * (share * inverse) for (context, _), share in zip(pieces, shares)]
    )
    return context, top + jnp.log(total) * LOG2E


def attend_kernel(layout, per, slots, keep, sends, order_ref, place_ref, own_key, own_value, cos_ref, sin_ref, q_ref, *rest):
    parts = sum(layout)
    received = list(rest[:parts])
    keep_ref, keep_log_ref = rest[parts : parts + 2]
    send_refs = rest[parts + 2 : parts + 2 + sends]
    key_scr, value_scr, score_scr, top_scr, context_scr, log_scr = rest[parts + 2 + sends :]
    rows = own_key.shape[0]
    blocks = len(layout)
    for block in range(blocks):
        here = [received.pop(0) for _ in range(layout[block])]
        for is_value in range(2):
            lanes = slice(is_value * HD, (is_value + 1) * HD)
            terms = [decode(part[:rows, lanes], part[rows:, lanes]) for part in here]
            if block == 0:
                terms = [(own_value if is_value else own_key)[...]] + terms
            whole = functools.reduce(jnp.add, terms)
            window = slice(block * rows, (block + 1) * rows)
            if is_value:
                value_scr[:HD, window] = jnp.transpose(whole).astype(jnp.bfloat16)
            else:
                whole = whole * cos_ref[window] + pltpu.roll(whole, HD // 2, 1) * sin_ref[window]
                key_scr[window] = whole.astype(jnp.bfloat16)
    value_scr[HD:] = jnp.ones((STAT_ROWS, blocks * rows), jnp.bfloat16)
    total_keys = blocks * rows
    tile = min(512, total_keys)

    def score(index, buffer):
        query = q_ref[order_ref[index]]
        tops = []
        for start in range(0, total_keys, tile):
            scores = jnp.dot(key_scr[start : start + tile], query, preferred_element_type=jnp.float32)
            score_scr[buffer, start : start + tile] = scores
            tops.append(jnp.max(scores, axis=0, keepdims=True))
        top = functools.reduce(jnp.maximum, tops) * TO_LOG2
        top_scr[buffer] = jnp.broadcast_to(top, top_scr.shape[1:])

    def weigh(index, buffer):
        top = top_scr[buffer][:1]
        summed = None
        for start in range(0, total_keys, tile):
            weights = jnp.exp2(score_scr[buffer, start : start + tile] * TO_LOG2 - top).astype(jnp.bfloat16)
            term = jnp.dot(value_scr[:, start : start + tile], weights, preferred_element_type=jnp.float32)
            summed = term if summed is None else summed + term
        total = summed[HD : HD + 1]
        context_scr[place_ref[index]] = summed[:HD] * (1.0 / total)
        log_scr[place_ref[index]] = jnp.broadcast_to(top + jnp.log(total) * LOG2E, log_scr.shape[1:])

    score(0, 0)

    @pl.loop(0, per // 2)
    def _(pair):
        score(2 * pair + 1, 1)
        weigh(2 * pair, 0)
        score(jnp.minimum(2 * pair + 2, per - 1), 0)
        weigh(2 * pair + 1, 1)

    @pl.loop(per, slots)
    def _(index):
        context_scr[place_ref[index]] = jnp.zeros(context_scr.shape[1:], jnp.float32)
        log_scr[place_ref[index]] = jnp.full(log_scr.shape[1:], EMPTY, jnp.float32)

    for slot in range(keep):
        keep_ref[slot] = context_scr[slot]
        keep_log_ref[slot] = log_scr[slot]
    for number, send_ref in enumerate(send_refs):
        for slot in range(keep):
            where = (number + 1) * keep + slot
            context, stats = pack(context_scr[where], log_scr[where][:1])
            send_ref[slot, :HD] = context
            send_ref[slot, HD:] = stats


def attend(order, place, own, cosine, sine, q_all, received, head, per, keep):
    rows = own[0].shape[0]
    slots, _, wide = q_all.shape
    blocks = len(received)
    layout = [len(parts) for parts in received]
    flat = [part for parts in received for part in parts]
    sends = slots // keep - 1

    def whole(shape):
        return pl.BlockSpec(shape, lambda i, a, b: (0,) * len(shape))

    shapes = [
        jax.ShapeDtypeStruct((keep, HD, wide), jnp.float32),
        jax.ShapeDtypeStruct((keep, 8, wide), jnp.float32),
    ] + [jax.ShapeDtypeStruct((keep, HD + STAT_ROWS, wide), jnp.bfloat16)] * sends
    return pl.pallas_call(
        functools.partial(attend_kernel, layout, per, slots, keep, sends),
        out_shape=tuple(shapes),
        grid_spec=pltpu.PrefetchScalarGridSpec(
            num_scalar_prefetch=2,
            grid=(1,),
            in_specs=[
                whole((rows, HD)),
                whole((rows, HD)),
                whole((blocks * rows, HD)),
                whole((blocks * rows, HD)),
                pl.BlockSpec((slots, HD, wide), lambda i, a, b: (0, head, 0)),
            ]
            + [whole(part.shape) for part in flat],
            out_specs=tuple(whole(shape.shape) for shape in shapes),
            scratch_shapes=[
                pltpu.VMEM((blocks * rows, HD), jnp.bfloat16),
                pltpu.VMEM((HD + STAT_ROWS, blocks * rows), jnp.bfloat16),
                pltpu.VMEM((2, blocks * rows, wide), jnp.float32),
                pltpu.VMEM((2, 8, wide), jnp.float32),
                pltpu.VMEM((slots, HD, wide), jnp.float32),
                pltpu.VMEM((slots, 8, wide), jnp.float32),
            ],
        ),
        compiler_params=pltpu.CompilerParams(vmem_limit_bytes=BIG),
        cost_estimate=pl.CostEstimate(
            flops=8 * per * blocks * rows * wide * HD,
            bytes_accessed=blocks * rows * HD * 16 + slots * HD * wide * 4,
            transcendentals=per * blocks * rows * wide,
        ),
        name="attend",
    )(order, place, *own, cosine, sine, q_all, *flat)


def gather_kernel(parts, keep_ref, keep_log_ref, *rest):
    received = rest[:parts]
    context_ref, log_ref = rest[parts : parts + 2]
    sends = rest[parts + 2 :]
    for slot in range(keep_ref.shape[0]):
        pieces = [(keep_ref[slot], keep_log_ref[slot][:1])] + [unpack(part[slot]) for part in received]
        context, logsum = blend(pieces)
        if slot == 0:
            context_ref[...] = context
            log_ref[...] = jnp.broadcast_to(logsum, log_ref.shape)
        else:
            packed, stats = pack(context, logsum)
            sends[slot - 1][:HD] = packed
            sends[slot - 1][HD:] = stats


def gather(keep, keep_log, received):
    count, _, wide = keep.shape
    shapes = [
        jax.ShapeDtypeStruct((HD, wide), jnp.float32),
        jax.ShapeDtypeStruct((8, wide), jnp.float32),
    ] + [jax.ShapeDtypeStruct((HD + STAT_ROWS, wide), jnp.bfloat16)] * (count - 1)
    outs = pl.pallas_call(
        functools.partial(gather_kernel, len(received)),
        out_shape=tuple(shapes),
        compiler_params=pltpu.CompilerParams(vmem_limit_bytes=BIG),
        cost_estimate=pl.CostEstimate(
            flops=4 * (len(received) + 1) * count * HD * wide,
            bytes_accessed=count * HD * wide * (6 + 2 * len(received)),
            transcendentals=0,
        ),
        name="gather",
    )(keep, keep_log, *received)
    return outs[0], outs[1], list(outs[2:])


def finish_kernel(split, context_ref, log_ref, *rest):
    received = rest[: 2 * split - 1]
    context_out, log_out = rest[2 * split - 1 :]
    for apart in range(split):
        pieces = []
        if apart == 0:
            pieces.append((context_ref[...], log_ref[:1]))
        else:
            pieces.append(unpack(received[apart - 1][...]))
        pieces.append(unpack(received[split - 1 + apart][...]))
        context, logsum = blend(pieces)
        context_out[apart] = jnp.transpose(context)
        log_out[apart] = jnp.broadcast_to(logsum, log_out.shape[1:])


def finish(context, log, received, split):
    wide = context.shape[1]
    return pl.pallas_call(
        functools.partial(finish_kernel, split),
        out_shape=(
            jax.ShapeDtypeStruct((split, wide, HD), jnp.float32),
            jax.ShapeDtypeStruct((split, 8, wide), jnp.float32),
        ),
        compiler_params=pltpu.CompilerParams(vmem_limit_bytes=BIG),
        cost_estimate=pl.CostEstimate(
            flops=8 * split * HD * wide, bytes_accessed=16 * split * HD * wide, transcendentals=0
        ),
        name="finish",
    )(context, log, *received)


def tables(starts, rows):
    half_width = HD // 2
    inverse_freq = 500000.0 ** (-(jnp.arange(half_width, dtype=jnp.float32) * 2.0 / HD))
    positions = (starts[:, None] + jnp.arange(rows, dtype=jnp.int32)[None, :]).reshape(-1)
    angles = positions.astype(jnp.float32)[:, None] * inverse_freq[None, :]
    cosine = jnp.cos(angles)
    sine = jnp.sin(angles)
    return jnp.concatenate([cosine, cosine], 1), jnp.concatenate([-sine, sine], 1)


def on_device(
    prefill_states,
    key_weight,
    value_weight,
    offsets,
    matching,
    queries,
    cache_keys,
    cache_values,
    cache_lengths,
):
    tp = lax.axis_size("tp")
    groups = lax.axis_size("grp")
    me = lax.axis_index("grp").astype(jnp.int32)
    rank = lax.axis_index("tp").astype(jnp.int32)
    block_len = prefill_states.shape[0]
    kv_local = key_weight.shape[1] // HD // tp
    row_count = queries.shape[0]
    group_size = queries.shape[1] // kv_local
    wide = row_count * group_size
    split = 2 if kv_local % 2 == 0 else 1
    chunks = kv_local // split
    per = groups // PROMPTS
    homes = per // split
    keep = PROMPTS * split
    core = me % split
    spot = (me // split) % homes
    side = me // per

    grouped = queries.reshape(row_count, kv_local, group_size, HD)
    turned = grouped.reshape(row_count, chunks, split, group_size, HD).transpose(2, 1, 4, 0, 3)
    turned = turned.reshape(split, chunks * HD, wide)
    line = jnp.arange(STAT_ROWS, dtype=jnp.int32)[None, :, None]
    tag = jnp.where(line == 0, matching[0], offsets[0]).astype(jnp.bfloat16)
    turned = jnp.concatenate([turned, jnp.broadcast_to(tag, (split, STAT_ROWS, wide))], 1)
    sorted_queries = [lax.dynamic_index_in_dim(turned, core ^ apart, 0, False) for apart in range(split)]
    own_queries = [sorted_queries[0]] + [
        lax.ppermute(sorted_queries[apart], "grp", [(i, i ^ apart) for i in range(groups)])
        for apart in range(1, split)
    ]
    def exchange(array, shift, apart):
        pairs = [
            (g * tp + t, (g ^ apart) * tp + (t + shift) % tp) for g in range(groups) for t in range(tp)
        ]
        return lax.ppermute(array, ("grp", "tp"), pairs)

    received = [[[] for _ in range(split)] for _ in range(chunks)]
    own = [None] * chunks

    def column(shift, chunk):
        return ((rank + shift) % tp) * chunks + chunk

    def run(jobs, core):
        results = project(
            prefill_states,
            key_weight,
            value_weight,
            core,
            [column(shift, chunk) for shift, chunk in jobs],
            ["own" if shift == 0 else "send" for shift, _ in jobs],
            split,
        )
        for (shift, chunk), outs in zip(jobs, results):
            if shift == 0:
                own[chunk] = outs[:2]
                outs = [None] + outs[2:]
            for apart in range(split):
                if outs[apart] is not None:
                    received[chunk][apart].append(exchange(outs[apart], shift, apart))

    jobs = [(shift, chunk) for chunk in range(chunks) for shift in range(1, tp)]
    run(jobs[:1], core)
    own_queries, later_core = lax.optimization_barrier((own_queries, core))
    members = [[chip * split + c for chip in range(groups // split)] for c in range(split)]
    q_all = lax.all_gather(jnp.stack(own_queries), "grp", axis_index_groups=members)
    q_all = q_all.reshape(groups, chunks * HD + STAT_ROWS, wide)
    wanted = q_all[:, chunks * HD, 0].astype(jnp.int32)
    starts = jnp.stack([own[chunks * HD + 1, 0] for own in own_queries]).astype(jnp.int32)
    run(jobs[1:] + [(0, chunk) for chunk in range(chunks)], later_core)

    cosine, sine = tables(starts, block_len)
    mine = (wanted == side).astype(jnp.int32)
    before = jnp.cumsum(mine)
    names = jnp.arange(groups, dtype=jnp.int32)
    target = jnp.where(mine == 1, before - 1, per + names - before)
    order = jnp.sum(jnp.where(target[None, :] == names[:, None], names[None, :], 0), 1).astype(jnp.int32)
    away = ((order // split) % homes) ^ spot
    place = (away * PROMPTS + ((order // per) ^ side)) * split + order % split

    grouped, own[-1] = lax.optimization_barrier((grouped, own[-1]))
    score_scale = HD ** (-0.5)
    cache_len = cache_keys.shape[2]
    cache_scores = (
        jnp.einsum("rkgd,rktd->rkgt", grouped, cache_keys, preferred_element_type=jnp.float32)
        * score_scale
    )
    alive = (jnp.arange(cache_len, dtype=jnp.int32)[None, :] < cache_lengths[:, None])[:, None, None, :]
    cache_scores = jnp.where(alive, cache_scores, EMPTY)
    cache_top = cache_scores.max(-1)
    cache_weights = jnp.where(alive, jnp.exp(cache_scores - cache_top[..., None]), 0.0)
    cache_total = cache_weights.sum(-1)
    cache_sum = jnp.einsum(
        "rkgt,rktd->rkgd",
        cache_weights.astype(jnp.bfloat16),
        cache_values,
        preferred_element_type=jnp.float32,
    )
    cache_sum, cache_total, cache_top, order, place = lax.optimization_barrier(
        (cache_sum, cache_total, cache_top, order, place)
    )

    def partner(i, side_apart, apart):
        return (i + side_apart * per) % groups ^ apart

    contexts = []
    logs = []
    for chunk in range(chunks):
        outs = attend(order, place, own[chunk], cosine, sine, q_all, received[chunk], chunk, per, keep)
        arrived = [
            lax.ppermute(outs[2 + far - 1], "grp", [(i, i ^ (far * split)) for i in range(groups)])
            for far in range(1, homes)
        ]
        context, log, sends = gather(outs[0], outs[1], arrived)
        final = [
            lax.ppermute(
                sends[number - 1],
                "grp",
                [(i, partner(i, number // split, number % split)) for i in range(groups)],
            )
            for number in range(1, keep)
        ]
        context, log = finish(context, log, final, split)
        contexts.append(context)
        logs.append(log[:, 0])
    contexts = jnp.stack(contexts)
    logs = jnp.stack(logs)
    if split == 2:
        contexts = jnp.where(core == 0, contexts, contexts[:, ::-1])
        logs = jnp.where(core == 0, logs, logs[:, ::-1])
    prompt_context = contexts.reshape(kv_local, row_count, group_size, HD).transpose(1, 0, 2, 3)
    prompt_log = logs.reshape(kv_local, row_count, group_size).transpose(1, 0, 2)
    cache_log = cache_top * LOG2E
    top = jnp.maximum(prompt_log, cache_log)
    prompt_share = jnp.exp2(prompt_log - top)
    cache_share = jnp.exp2(cache_log - top)
    total = prompt_share + cache_share * cache_total
    context = (prompt_context * prompt_share[..., None] + cache_sum * cache_share[..., None]) / total[..., None]
    return context.reshape(row_count, kv_local * group_size, HD).astype(jnp.bfloat16)


def solution(mesh):
    placed = (
        P("grp", "tp"),
        P("tp", None),
        P("tp", None),
        P("grp"),
        P("grp"),
        P("grp", "tp", None),
        P("grp", "tp", None, None),
        P("grp", "tp", None, None),
        P("grp"),
    )
    return jax.shard_map(
        on_device, mesh=mesh, in_specs=placed, out_specs=P("grp", "tp", None), check_vma=False
    )
```

```python
import functools

import jax
import jax.numpy as jnp
from jax import lax
from jax.experimental import pallas as pl
from jax.experimental.pallas import tpu as pltpu
from jax.sharding import PartitionSpec as P

HD = 128
PROMPTS = 2
CODE_BLOCKS = 16
CODE_TOP = 32000.0
STAT_ROWS = 16
EMPTY = -1e30
LOG2E = 1.4426950408889634
TO_LOG2 = HD ** (-0.5) * LOG2E
BIG = 60 * 1024 * 1024
SMALL = 16 * 1024 * 1024
ANY = pl.BlockSpec(memory_space=pl.ANY)


def encode(values):
    rows = values.shape[0]
    blocks = values.reshape(CODE_BLOCKS, rows // CODE_BLOCKS, HD)
    largest = jnp.maximum(jnp.max(jnp.abs(blocks), axis=1), 1e-30)
    exponent = jnp.floor(jnp.log(largest) * LOG2E) + 1.0
    factor = jnp.exp2(-exponent) * CODE_TOP
    codes = (blocks * factor[:, None, :]).astype(jnp.int32).astype(jnp.int16)
    return codes.reshape(rows, HD), exponent.astype(jnp.int32).astype(jnp.int16)


def decode(codes, exponent):
    rows = codes.shape[0]
    factor = jnp.exp2(exponent.astype(jnp.int32).astype(jnp.float32)) * (1.0 / CODE_TOP)
    blocks = codes.astype(jnp.int32).astype(jnp.float32).reshape(CODE_BLOCKS, rows // CODE_BLOCKS, HD)
    return (blocks * factor[:, None, :]).reshape(rows, HD)


def project_kernel(plan, split, pieces, place_ref, x_hbm, wk_ref, wv_ref, *rest):
    count = sum(split - (kind == "own") for kind in plan) + 2 * plan.count("own")
    outs = rest[:count]
    x_ref, acc, sems = rest[count:]
    step = pl.program_id(0)
    rows = x_ref.shape[0]
    width = wk_ref.shape[1]
    part = rows // pieces

    def fetch(piece):
        window = pl.ds(piece * part, part)
        return pltpu.make_async_copy(x_hbm.at[window], x_ref.at[window], sems.at[piece])

    @pl.when(step == 0)
    def _():
        for piece in range(pieces):
            fetch(piece).start()

    for piece in range(pieces):

        @pl.when(step == 0)
        def _():
            fetch(piece).wait()

        window = pl.ds(piece * part, part)
        acc[window, :width] = jnp.dot(x_ref[window], wk_ref[...], preferred_element_type=jnp.float32)
        acc[window, width:] = jnp.dot(x_ref[window], wv_ref[...], preferred_element_type=jnp.float32)

    core = place_ref[0]
    index = 0
    for number, kind in enumerate(plan):
        here = list(outs[index : index + split + (kind == "own")])
        index += split + (kind == "own")

        @pl.when(step == number)
        def _():
            refs = list(here)
            for apart in range(split):
                lanes = pl.multiple_of((core ^ apart) * HD, HD)
                if kind == "own" and apart == 0:
                    refs.pop(0)[...] = acc[:, pl.ds(lanes, HD)]
                    refs.pop(0)[...] = acc[:, pl.ds(width + lanes, HD)]
                    continue
                ref = refs.pop(0)
                for half in range(2):
                    codes, exponent = encode(acc[:, pl.ds(half * width + lanes, HD)])
                    ref[:rows, half * HD : (half + 1) * HD] = codes
                    ref[rows:, half * HD : (half + 1) * HD] = exponent


def project(x, wk, wv, core, columns, plan, split):
    rows, depth = x.shape
    width = split * HD
    steps = len(plan)
    pieces = 2
    coded = jax.ShapeDtypeStruct((rows + CODE_BLOCKS, 2 * HD), jnp.int16)
    plain = jax.ShapeDtypeStruct((rows, HD), jnp.float32)
    shapes = []
    for kind in plan:
        shapes += ([plain, plain] if kind == "own" else [coded]) + [coded] * (split - 1)
    weight_spec = pl.BlockSpec((depth, width), lambda s, p: (0, p[1 + s]))
    place = jnp.stack([core] + columns).astype(jnp.int32)
    outs = pl.pallas_call(
        functools.partial(project_kernel, plan, split, pieces),
        out_shape=tuple(shapes),
        grid_spec=pltpu.PrefetchScalarGridSpec(
            num_scalar_prefetch=1,
            grid=(steps,),
            in_specs=[ANY, weight_spec, weight_spec],
            out_specs=tuple(pl.BlockSpec(shape.shape, lambda s, p: (0, 0)) for shape in shapes),
            scratch_shapes=[
                pltpu.VMEM((rows, depth), x.dtype),
                pltpu.VMEM((rows, 2 * width), jnp.float32),
                pltpu.SemaphoreType.DMA((pieces,)),
            ],
        ),
        compiler_params=pltpu.CompilerParams(vmem_limit_bytes=BIG),
        cost_estimate=pl.CostEstimate(
            flops=4 * rows * depth * width * steps,
            bytes_accessed=2 * rows * depth + steps * (4 * depth * width + 4 * rows * width),
            transcendentals=0,
        ),
        name="project",
    )(place, x, wk, wv)
    results = []
    index = 0
    for kind in plan:
        size = split + (kind == "own")
        results.append(list(outs[index : index + size]))
        index += size
    return results


def pack(context, logsum):
    high = logsum.astype(jnp.bfloat16).astype(jnp.float32)
    middle = (logsum - high).astype(jnp.bfloat16).astype(jnp.float32)
    low = logsum - high - middle
    line = lax.broadcasted_iota(jnp.int32, (STAT_ROWS, context.shape[1]), 0)
    stats = jnp.where(line == 0, high, jnp.where(line == 1, middle, jnp.where(line == 2, low, 0.0)))
    return context.astype(jnp.bfloat16), stats.astype(jnp.bfloat16)


def unpack(block):
    stats = block[HD:].astype(jnp.float32)
    return block[:HD].astype(jnp.float32), stats[0:1] + stats[1:2] + stats[2:3]


def blend(pieces):
    top = functools.reduce(jnp.maximum, [logsum for _, logsum in pieces])
    shares = [jnp.exp2(logsum - top) for _, logsum in pieces]
    total = functools.reduce(jnp.add, shares)
    inverse = 1.0 / total
    context = functools.reduce(
        jnp.add, [context * (share * inverse) for (context, _), share in zip(pieces, shares)]
    )
    return context, top + jnp.log(total) * LOG2E


def attend_kernel(layout, per, slots, keep, sends, order_ref, place_ref, own_key, own_value, turn_ref, q_ref, *rest):
    parts = sum(layout)
    received = list(rest[:parts])
    keep_ref, keep_log_ref = rest[parts : parts + 2]
    send_refs = rest[parts + 2 : parts + 2 + sends]
    key_scr, value_scr, score_scr, top_scr, context_scr, log_scr = rest[parts + 2 + sends :]
    rows = own_key.shape[0]
    blocks = len(layout)
    for block in range(blocks):
        here = [received.pop(0) for _ in range(layout[block])]
        for is_value in range(2):
            lanes = slice(is_value * HD, (is_value + 1) * HD)
            terms = [decode(part[:rows, lanes], part[rows:, lanes]) for part in here]
            if block == 0:
                terms = [(own_value if is_value else own_key)[...]] + terms
            whole = functools.reduce(jnp.add, terms)
            window = slice(block * rows, (block + 1) * rows)
            if is_value:
                value_scr[:HD, window] = jnp.transpose(whole).astype(jnp.bfloat16)
            else:
                turn = turn_ref[window]
                turned = pltpu.roll(turn, HD // 2, 1)
                low = lax.broadcasted_iota(jnp.int32, turn.shape, 1) < HD // 2
                cosine = jnp.where(low, turn, turned)
                sine = jnp.where(low, -turned, turn)
                whole = whole * cosine + pltpu.roll(whole, HD // 2, 1) * sine
                key_scr[window] = whole.astype(jnp.bfloat16)
    value_scr[HD:] = jnp.ones((STAT_ROWS, blocks * rows), jnp.bfloat16)
    total_keys = blocks * rows
    tile = min(512, total_keys)

    def score(index, buffer):
        query = q_ref[order_ref[index]]
        tops = []
        for start in range(0, total_keys, tile):
            scores = jnp.dot(key_scr[start : start + tile], query, preferred_element_type=jnp.float32)
            score_scr[buffer, start : start + tile] = scores
            tops.append(jnp.max(scores, axis=0, keepdims=True))
        top = functools.reduce(jnp.maximum, tops) * TO_LOG2
        top_scr[buffer] = jnp.broadcast_to(top, top_scr.shape[1:])

    def weigh(index, buffer):
        top = top_scr[buffer][:1]
        summed = None
        for start in range(0, total_keys, tile):
            weights = jnp.exp2(score_scr[buffer, start : start + tile] * TO_LOG2 - top).astype(jnp.bfloat16)
            term = jnp.dot(value_scr[:, start : start + tile], weights, preferred_element_type=jnp.float32)
            summed = term if summed is None else summed + term
        total = summed[HD : HD + 1]
        context_scr[place_ref[index]] = summed[:HD] * (1.0 / total)
        log_scr[place_ref[index]] = jnp.broadcast_to(top + jnp.log(total) * LOG2E, log_scr.shape[1:])

    score(0, 0)

    @pl.loop(0, per // 2)
    def _(pair):
        score(2 * pair + 1, 1)
        weigh(2 * pair, 0)
        score(jnp.minimum(2 * pair + 2, per - 1), 0)
        weigh(2 * pair + 1, 1)

    @pl.loop(per, slots)
    def _(index):
        context_scr[place_ref[index]] = jnp.zeros(context_scr.shape[1:], jnp.float32)
        log_scr[place_ref[index]] = jnp.full(log_scr.shape[1:], EMPTY, jnp.float32)

    for slot in range(keep):
        keep_ref[slot] = context_scr[slot]
        keep_log_ref[slot] = log_scr[slot]
    for number, send_ref in enumerate(send_refs):
        for slot in range(keep):
            where = (number + 1) * keep + slot
            context, stats = pack(context_scr[where], log_scr[where][:1])
            send_ref[slot, :HD] = context
            send_ref[slot, HD:] = stats


def attend(order, place, own, turn, q_all, received, head, per, keep):
    rows = own[0].shape[0]
    slots, _, wide = q_all.shape
    blocks = len(received)
    layout = [len(parts) for parts in received]
    flat = [part for parts in received for part in parts]
    sends = slots // keep - 1

    def whole(shape):
        return pl.BlockSpec(shape, lambda i, a, b: (0,) * len(shape))

    shapes = [
        jax.ShapeDtypeStruct((keep, HD, wide), jnp.float32),
        jax.ShapeDtypeStruct((keep, 8, wide), jnp.float32),
    ] + [jax.ShapeDtypeStruct((keep, HD + STAT_ROWS, wide), jnp.bfloat16)] * sends
    return pl.pallas_call(
        functools.partial(attend_kernel, layout, per, slots, keep, sends),
        out_shape=tuple(shapes),
        grid_spec=pltpu.PrefetchScalarGridSpec(
            num_scalar_prefetch=2,
            grid=(1,),
            in_specs=[
                whole((rows, HD)),
                whole((rows, HD)),
                whole((blocks * rows, HD)),
                pl.BlockSpec((slots, HD, wide), lambda i, a, b: (0, head + a[slots], 0)),
            ]
            + [whole(part.shape) for part in flat],
            out_specs=tuple(whole(shape.shape) for shape in shapes),
            scratch_shapes=[
                pltpu.VMEM((blocks * rows, HD), jnp.bfloat16),
                pltpu.VMEM((HD + STAT_ROWS, blocks * rows), jnp.bfloat16),
                pltpu.VMEM((2, blocks * rows, wide), jnp.float32),
                pltpu.VMEM((2, 8, wide), jnp.float32),
                pltpu.VMEM((slots, HD, wide), jnp.float32),
                pltpu.VMEM((slots, 8, wide), jnp.float32),
            ],
        ),
        compiler_params=pltpu.CompilerParams(vmem_limit_bytes=2 * SMALL),
        cost_estimate=pl.CostEstimate(
            flops=8 * per * blocks * rows * wide * HD,
            bytes_accessed=blocks * rows * HD * 16 + slots * HD * wide * 4,
            transcendentals=per * blocks * rows * wide,
        ),
        name="attend",
    )(order, place, *own, turn, q_all, *flat)


def gather_kernel(parts, keep_ref, keep_log_ref, *rest):
    received = rest[:parts]
    context_ref, log_ref = rest[parts : parts + 2]
    sends = rest[parts + 2 :]
    for slot in range(keep_ref.shape[0]):
        pieces = [(keep_ref[slot], keep_log_ref[slot][:1])] + [unpack(part[slot]) for part in received]
        context, logsum = blend(pieces)
        if slot == 0:
            context_ref[...] = context
            log_ref[...] = jnp.broadcast_to(logsum, log_ref.shape)
        else:
            packed, stats = pack(context, logsum)
            sends[slot - 1][:HD] = packed
            sends[slot - 1][HD:] = stats


def gather(keep, keep_log, received):
    count, _, wide = keep.shape
    shapes = [
        jax.ShapeDtypeStruct((HD, wide), jnp.float32),
        jax.ShapeDtypeStruct((8, wide), jnp.float32),
    ] + [jax.ShapeDtypeStruct((HD + STAT_ROWS, wide), jnp.bfloat16)] * (count - 1)
    outs = pl.pallas_call(
        functools.partial(gather_kernel, len(received)),
        out_shape=tuple(shapes),
        compiler_params=pltpu.CompilerParams(vmem_limit_bytes=SMALL),
        cost_estimate=pl.CostEstimate(
            flops=4 * (len(received) + 1) * count * HD * wide,
            bytes_accessed=count * HD * wide * (6 + 2 * len(received)),
            transcendentals=0,
        ),
        name="gather",
    )(keep, keep_log, *received)
    return outs[0], outs[1], list(outs[2:])


def finish_kernel(split, aliased, core_ref, context_ref, log_ref, *rest):
    received = rest[: 2 * split - 1]
    cache_ref, cache_log_ref = rest[2 * split - 1 : 2 * split + 1]
    out_ref = rest[2 * split + 1 + aliased]
    core = core_ref[0]
    rows, heads = out_ref.shape[:2]
    done = []
    for apart in range(split):
        pieces = []
        if apart == 0:
            pieces.append((context_ref[...], log_ref[:1]))
        else:
            pieces.append(unpack(received[apart - 1][...]))
        pieces.append(unpack(received[split - 1 + apart][...]))
        pieces.append((cache_ref[core ^ apart], cache_log_ref[core ^ apart][:1]))
        context, _ = blend(pieces)
        done.append(jnp.transpose(context).reshape(rows, heads // split, HD))
    if split == 2:
        first = jnp.where(core == 0, done[0], done[1])
        second = jnp.where(core == 0, done[1], done[0])
        done = [jnp.concatenate([first, second], 1)]
    out_ref[...] = done[0].astype(out_ref.dtype)


def finish(core, context, log, received, cache, cache_log, split, chunk, shape, before):
    wide = context.shape[1]
    rows, all_heads, _ = shape
    part = all_heads * split // cache.shape[0]

    def whole(array):
        return pl.BlockSpec(array.shape, lambda i, c: (0,) * array.ndim)

    operands = [context, log, *received]
    specs = [whole(array) for array in operands]
    operands += [cache, cache_log]
    specs += [
        pl.BlockSpec((split, HD, wide), lambda i, c: (chunk, 0, 0)),
        pl.BlockSpec((split, 8, wide), lambda i, c: (chunk, 0, 0)),
    ]
    aliases = {}
    if before is not None:
        operands.append(before)
        specs.append(ANY)
        aliases = {len(operands): 0}
    return pl.pallas_call(
        functools.partial(finish_kernel, split, before is not None),
        out_shape=jax.ShapeDtypeStruct(shape, jnp.bfloat16),
        grid_spec=pltpu.PrefetchScalarGridSpec(
            num_scalar_prefetch=1,
            grid=(1,),
            in_specs=specs,
            out_specs=pl.BlockSpec((rows, part, HD), lambda i, c: (0, chunk, 0)),
        ),
        input_output_aliases=aliases,
        compiler_params=pltpu.CompilerParams(vmem_limit_bytes=SMALL),
        cost_estimate=pl.CostEstimate(
            flops=8 * split * HD * wide, bytes_accessed=16 * split * HD * wide, transcendentals=0
        ),
        name="finish",
    )(core.reshape(1), *operands)


def tables(starts, rows):
    half_width = HD // 2
    inverse_freq = 500000.0 ** (-(jnp.arange(half_width, dtype=jnp.float32) * 2.0 / HD))
    positions = (starts[:, None] + jnp.arange(rows, dtype=jnp.int32)[None, :]).reshape(-1)
    angles = positions.astype(jnp.float32)[:, None] * inverse_freq[None, :]
    cosine = jnp.cos(angles)
    sine = jnp.sin(angles)
    return jnp.concatenate([cosine, sine], 1)


def on_device(
    prefill_states,
    key_weight,
    value_weight,
    offsets,
    matching,
    queries,
    cache_keys,
    cache_values,
    cache_lengths,
):
    tp = lax.axis_size("tp")
    groups = lax.axis_size("grp")
    me = lax.axis_index("grp").astype(jnp.int32)
    rank = lax.axis_index("tp").astype(jnp.int32)
    block_len = prefill_states.shape[0]
    kv_local = key_weight.shape[1] // HD // tp
    row_count = queries.shape[0]
    group_size = queries.shape[1] // kv_local
    wide = row_count * group_size
    split = 2 if kv_local % 2 == 0 else 1
    chunks = kv_local // split
    per = groups // PROMPTS
    homes = per // split
    keep = PROMPTS * split
    core = me % split
    spot = (me // split) % homes
    side = me // per

    grouped = queries.reshape(row_count, kv_local, group_size, HD)
    turned = grouped.transpose(1, 3, 0, 2).reshape(kv_local * HD, wide)
    tag = jnp.broadcast_to(matching[0].astype(jnp.bfloat16), (STAT_ROWS, wide))
    q_all = lax.all_gather(jnp.concatenate([turned, tag], 0), "grp")
    wanted = q_all[:, kv_local * HD, 0].astype(jnp.int32)
    starts = [offsets] + [
        lax.ppermute(offsets, "grp", [(i, i ^ apart) for i in range(groups)]) for apart in range(1, split)
    ]

    def exchange(array, shift, apart):
        pairs = [
            (g * tp + t, (g ^ apart) * tp + (t + shift) % tp) for g in range(groups) for t in range(tp)
        ]
        return lax.ppermute(array, ("grp", "tp"), pairs)

    received = [[[] for _ in range(split)] for _ in range(chunks)]
    own = [None] * chunks

    def column(shift, chunk):
        return ((rank + shift) % tp) * chunks + chunk

    def run(jobs, core):
        results = project(
            prefill_states,
            key_weight,
            value_weight,
            core,
            [column(shift, chunk) for shift, chunk in jobs],
            ["own" if shift == 0 else "send" for shift, _ in jobs],
            split,
        )
        results, core = lax.optimization_barrier((results, core))
        for (shift, chunk), outs in zip(jobs, results):
            if shift == 0:
                own[chunk] = outs[:2]
                outs = [None] + outs[2:]
            for apart in range(split):
                if outs[apart] is not None:
                    received[chunk][apart].append(exchange(outs[apart], shift, apart))
        return core

    jobs = [(shift, chunk) for chunk in range(chunks) for shift in range(1, tp)]
    later = run(jobs[:1], core)
    run(jobs[1:] + [(0, chunk) for chunk in range(chunks)], later)

    turn = tables(jnp.concatenate(starts), block_len)
    mine = (wanted == side).astype(jnp.int32)
    before = jnp.cumsum(mine)
    names = jnp.arange(groups, dtype=jnp.int32)
    target = jnp.where(mine == 1, before - 1, per + names - before)
    order = jnp.sum(jnp.where(target[None, :] == names[:, None], names[None, :], 0), 1).astype(jnp.int32)
    away = ((order // split) % homes) ^ spot
    place = (away * PROMPTS + ((order // per) ^ side)) * split + (order % split ^ core)
    order = jnp.concatenate([order, core.reshape(1)])

    grouped, own[-1] = lax.optimization_barrier((grouped, own[-1]))
    score_scale = HD ** (-0.5)
    cache_len = cache_keys.shape[2]
    cache_scores = (
        jnp.einsum("rkgd,rktd->rkgt", grouped, cache_keys, preferred_element_type=jnp.float32)
        * score_scale
    )
    alive = (jnp.arange(cache_len, dtype=jnp.int32)[None, :] < cache_lengths[:, None])[:, None, None, :]
    cache_scores = jnp.where(alive, cache_scores, EMPTY)
    cache_top = cache_scores.max(-1)
    cache_weights = jnp.where(alive, jnp.exp(cache_scores - cache_top[..., None]), 0.0)
    cache_total = cache_weights.sum(-1)
    cache_sum = jnp.einsum(
        "rkgt,rktd->rkgd",
        cache_weights.astype(jnp.bfloat16),
        cache_values,
        preferred_element_type=jnp.float32,
    )
    cache_context = cache_sum / cache_total[..., None]
    cache_context = cache_context.transpose(1, 3, 0, 2).reshape(kv_local, HD, wide)
    cache_log = cache_top * LOG2E + jnp.log2(cache_total)
    cache_log = cache_log.transpose(1, 0, 2).reshape(kv_local, 1, wide)
    cache_log = jnp.broadcast_to(cache_log, (kv_local, 8, wide))
    cache_context, cache_log, order, place = lax.optimization_barrier((cache_context, cache_log, order, place))

    def partner(i, side_apart, apart):
        return (i + side_apart * per) % groups ^ apart

    result = None
    for chunk in range(chunks):
        outs = attend(order, place, own[chunk], turn, q_all, received[chunk], chunk * split, per, keep)
        outs, order = lax.optimization_barrier((outs, order))
        arrived = [
            lax.ppermute(outs[2 + far - 1], "grp", [(i, i ^ (far * split)) for i in range(groups)])
            for far in range(1, homes)
        ]
        context, log, sends = gather(outs[0], outs[1], arrived)
        final = [
            lax.ppermute(
                sends[number - 1],
                "grp",
                [(i, partner(i, number // split, number % split)) for i in range(groups)],
            )
            for number in range(1, keep)
        ]
        result = finish(
            core, context, log, final, cache_context, cache_log, split, chunk, queries.shape, result
        )
    return result


def solution(mesh):
    placed = (
        P("grp", "tp"),
        P("tp", None),
        P("tp", None),
        P("grp"),
        P("grp"),
        P("grp", "tp", None),
        P("grp", "tp", None, None),
        P("grp", "tp", None, None),
        P("grp"),
    )
    return jax.shard_map(
        on_device, mesh=mesh, in_specs=placed, out_specs=P("grp", "tp", None), check_vma=False
    )
```

```python
import functools

import jax
import jax.numpy as jnp
from jax import lax
from jax.experimental import pallas as pl
from jax.experimental.pallas import tpu as pltpu
from jax.sharding import PartitionSpec as P

HD = 128
PROMPTS = 2
CODE_BLOCKS = 16
CODE_TOP = 32000.0
STAT_ROWS = 16
EMPTY = -1e30
LOG2E = 1.4426950408889634
TO_LOG2 = HD ** (-0.5) * LOG2E
BIG = 60 * 1024 * 1024
SMALL = 16 * 1024 * 1024
ANY = pl.BlockSpec(memory_space=pl.ANY)


def encode(values):
    rows = values.shape[0]
    blocks = values.reshape(CODE_BLOCKS, rows // CODE_BLOCKS, HD)
    largest = jnp.maximum(jnp.max(jnp.abs(blocks), axis=1), 1e-30)
    exponent = jnp.floor(jnp.log(largest) * LOG2E) + 1.0
    factor = jnp.exp2(-exponent) * CODE_TOP
    codes = (blocks * factor[:, None, :]).astype(jnp.int32).astype(jnp.int16)
    return codes.reshape(rows, HD), exponent.astype(jnp.int32).astype(jnp.int16)


def decode(codes, exponent):
    rows = codes.shape[0]
    factor = jnp.exp2(exponent.astype(jnp.int32).astype(jnp.float32)) * (1.0 / CODE_TOP)
    blocks = codes.astype(jnp.int32).astype(jnp.float32).reshape(CODE_BLOCKS, rows // CODE_BLOCKS, HD)
    return (blocks * factor[:, None, :]).reshape(rows, HD)


def project_kernel(plan, split, pieces, place_ref, x_hbm, wk_hbm, wv_hbm, *rest):
    count = sum(split - (kind == "own") for kind in plan) + 2 * plan.count("own")
    outs = list(rest[:count])
    x_ref, wk_ref, wv_ref, acc, x_sems, wk_sems, wv_sems = rest[count:]
    rows, depth = x_ref.shape
    width = wk_ref.shape[2]
    part = depth // pieces
    core = place_ref[0]

    def x_copy(piece):
        window = pl.ds(pl.multiple_of(piece * part, part), part)
        return pltpu.make_async_copy(x_hbm.at[:, window], x_ref.at[:, window], x_sems.at[piece])

    def weight_copies(step, piece):
        window = pl.ds(pl.multiple_of(piece * part, part), part)
        lanes = pl.ds(pl.multiple_of(place_ref[1 + step] * width, width), width)
        return [
            pltpu.make_async_copy(hbm.at[window, lanes], ref.at[step % 2, window], sems.at[step % 2, piece])
            for hbm, ref, sems in ((wk_hbm, wk_ref, wk_sems), (wv_hbm, wv_ref, wv_sems))
        ]

    for piece in range(pieces):
        x_copy(piece).start()
        for copy in weight_copies(0, piece):
            copy.start()
    for step, kind in enumerate(plan):
        if step + 1 < len(plan):
            for piece in range(pieces):
                for copy in weight_copies(step + 1, piece):
                    copy.start()

        for piece in range(pieces):
            if step == 0:
                x_copy(piece).wait()
            for copy in weight_copies(step, piece):
                copy.wait()
            window = slice(piece * part, (piece + 1) * part)
            left = x_ref[:, window]
            for half, ref in ((0, wk_ref), (1, wv_ref)):
                lanes = slice(half * width, (half + 1) * width)
                term = jnp.dot(left, ref[step % 2, window], preferred_element_type=jnp.float32)
                if piece == 0:
                    acc[:, lanes] = term
                else:
                    acc[:, lanes] += term
        for apart in range(split):
            lanes = pl.multiple_of((core ^ apart) * HD, HD)
            if kind == "own" and apart == 0:
                outs.pop(0)[...] = acc[:, pl.ds(lanes, HD)]
                outs.pop(0)[...] = acc[:, pl.ds(width + lanes, HD)]
                continue
            ref = outs.pop(0)
            for half in range(2):
                codes, exponent = encode(acc[:, pl.ds(half * width + lanes, HD)])
                ref[:rows, half * HD : (half + 1) * HD] = codes
                ref[rows:, half * HD : (half + 1) * HD] = exponent


def project(x, wk, wv, core, columns, plan, split):
    rows, depth = x.shape
    width = split * HD
    steps = len(plan)
    pieces = 4
    coded = jax.ShapeDtypeStruct((rows + CODE_BLOCKS, 2 * HD), jnp.int16)
    plain = jax.ShapeDtypeStruct((rows, HD), jnp.float32)
    shapes = []
    for kind in plan:
        shapes += ([plain, plain] if kind == "own" else [coded]) + [coded] * (split - 1)
    place = jnp.stack([core] + columns).astype(jnp.int32)
    outs = pl.pallas_call(
        functools.partial(project_kernel, plan, split, pieces),
        out_shape=tuple(shapes),
        grid_spec=pltpu.PrefetchScalarGridSpec(
            num_scalar_prefetch=1,
            grid=(1,),
            in_specs=[ANY, ANY, ANY],
            out_specs=tuple(pl.BlockSpec(shape.shape, lambda s, p: (0, 0)) for shape in shapes),
            scratch_shapes=[
                pltpu.VMEM((rows, depth), x.dtype),
                pltpu.VMEM((2, depth, width), wk.dtype),
                pltpu.VMEM((2, depth, width), wv.dtype),
                pltpu.VMEM((rows, 2 * width), jnp.float32),
                pltpu.SemaphoreType.DMA((pieces,)),
                pltpu.SemaphoreType.DMA((2, pieces)),
                pltpu.SemaphoreType.DMA((2, pieces)),
            ],
        ),
        compiler_params=pltpu.CompilerParams(vmem_limit_bytes=BIG),
        cost_estimate=pl.CostEstimate(
            flops=4 * rows * depth * width * steps,
            bytes_accessed=2 * rows * depth + steps * (4 * depth * width + 4 * rows * width),
            transcendentals=0,
        ),
        name="project",
    )(place, x, wk, wv)
    results = []
    index = 0
    for kind in plan:
        size = split + (kind == "own")
        results.append(list(outs[index : index + size]))
        index += size
    return results


def pack(context, logsum):
    high = logsum.astype(jnp.bfloat16).astype(jnp.float32)
    middle = (logsum - high).astype(jnp.bfloat16).astype(jnp.float32)
    low = logsum - high - middle
    line = lax.broadcasted_iota(jnp.int32, (STAT_ROWS, context.shape[1]), 0)
    stats = jnp.where(line == 0, high, jnp.where(line == 1, middle, jnp.where(line == 2, low, 0.0)))
    return context.astype(jnp.bfloat16), stats.astype(jnp.bfloat16)


def unpack(block):
    stats = block[HD:].astype(jnp.float32)
    return block[:HD].astype(jnp.float32), stats[0:1] + stats[1:2] + stats[2:3]


def blend(pieces):
    top = functools.reduce(jnp.maximum, [logsum for _, logsum in pieces])
    shares = [jnp.exp2(logsum - top) for _, logsum in pieces]
    total = functools.reduce(jnp.add, shares)
    inverse = 1.0 / total
    context = functools.reduce(
        jnp.add, [context * (share * inverse) for (context, _), share in zip(pieces, shares)]
    )
    return context, top + jnp.log(total) * LOG2E


def attend_kernel(layout, per, slots, keep, sends, order_ref, place_ref, own_key, own_value, cos_ref, sin_ref, q_ref, *rest):
    parts = sum(layout)
    received = list(rest[:parts])
    keep_ref, keep_log_ref = rest[parts : parts + 2]
    send_refs = rest[parts + 2 : parts + 2 + sends]
    key_scr, value_scr, score_scr, top_scr, context_scr, log_scr = rest[parts + 2 + sends :]
    rows = own_key.shape[0]
    blocks = len(layout)
    for block in range(blocks):
        here = [received.pop(0) for _ in range(layout[block])]
        for is_value in range(2):
            lanes = slice(is_value * HD, (is_value + 1) * HD)
            terms = [decode(part[:rows, lanes], part[rows:, lanes]) for part in here]
            if block == 0:
                terms = [(own_value if is_value else own_key)[...]] + terms
            whole = functools.reduce(jnp.add, terms)
            window = slice(block * rows, (block + 1) * rows)
            if is_value:
                value_scr[:HD, window] = jnp.transpose(whole).astype(jnp.bfloat16)
            else:
                cosine = cos_ref[...]
                sine = sin_ref[...]
                low = lax.broadcasted_iota(jnp.int32, cosine.shape, 1) < HD // 2
                mine = low if block == 0 else ~low
                cosine = jnp.where(mine, cosine, pltpu.roll(cosine, HD // 2, 1))
                sine = jnp.where(mine, sine, pltpu.roll(sine, HD // 2, 1))
                sine = jnp.where(low, -sine, sine)
                whole = whole * cosine + pltpu.roll(whole, HD // 2, 1) * sine
                key_scr[window] = whole.astype(jnp.bfloat16)
    value_scr[HD:] = jnp.ones((STAT_ROWS, blocks * rows), jnp.bfloat16)
    total_keys = blocks * rows
    tile = min(512, total_keys)

    def score(index, buffer):
        query = q_ref[order_ref[index]]
        tops = []
        for start in range(0, total_keys, tile):
            scores = jnp.dot(key_scr[start : start + tile], query, preferred_element_type=jnp.float32)
            score_scr[buffer, start : start + tile] = scores
            tops.append(jnp.max(scores, axis=0, keepdims=True))
        top = functools.reduce(jnp.maximum, tops) * TO_LOG2
        top_scr[buffer] = jnp.broadcast_to(top, top_scr.shape[1:])

    def weigh(index, buffer):
        top = top_scr[buffer][:1]
        summed = None
        for start in range(0, total_keys, tile):
            weights = jnp.exp2(score_scr[buffer, start : start + tile] * TO_LOG2 - top).astype(jnp.bfloat16)
            term = jnp.dot(value_scr[:, start : start + tile], weights, preferred_element_type=jnp.float32)
            summed = term if summed is None else summed + term
        total = summed[HD : HD + 1]
        context_scr[place_ref[index]] = summed[:HD] * (1.0 / total)
        log_scr[place_ref[index]] = jnp.broadcast_to(top + jnp.log(total) * LOG2E, log_scr.shape[1:])

    score(0, 0)

    @pl.loop(0, per // 2)
    def _(pair):
        score(2 * pair + 1, 1)
        weigh(2 * pair, 0)
        score(jnp.minimum(2 * pair + 2, per - 1), 0)
        weigh(2 * pair + 1, 1)

    @pl.loop(per, slots)
    def _(index):
        context_scr[place_ref[index]] = jnp.zeros(context_scr.shape[1:], jnp.float32)
        log_scr[place_ref[index]] = jnp.full(log_scr.shape[1:], EMPTY, jnp.float32)

    for slot in range(keep):
        keep_ref[slot] = context_scr[slot]
        keep_log_ref[slot] = log_scr[slot]
    for number, send_ref in enumerate(send_refs):
        for slot in range(keep):
            where = (number + 1) * keep + slot
            context, stats = pack(context_scr[where], log_scr[where][:1])
            send_ref[slot, :HD] = context
            send_ref[slot, HD:] = stats


def attend(order, place, own, cosine, sine, q_all, received, head, per, keep):
    rows = own[0].shape[0]
    slots, _, wide = q_all.shape
    blocks = len(received)
    layout = [len(parts) for parts in received]
    flat = [part for parts in received for part in parts]
    sends = slots // keep - 1

    def whole(shape):
        return pl.BlockSpec(shape, lambda i, a, b: (0,) * len(shape))

    shapes = [
        jax.ShapeDtypeStruct((keep, HD, wide), jnp.float32),
        jax.ShapeDtypeStruct((keep, 8, wide), jnp.float32),
    ] + [jax.ShapeDtypeStruct((keep, HD + STAT_ROWS, wide), jnp.bfloat16)] * sends
    return pl.pallas_call(
        functools.partial(attend_kernel, layout, per, slots, keep, sends),
        out_shape=tuple(shapes),
        grid_spec=pltpu.PrefetchScalarGridSpec(
            num_scalar_prefetch=2,
            grid=(1,),
            in_specs=[
                whole((rows, HD)),
                whole((rows, HD)),
                whole((rows, HD)),
                whole((rows, HD)),
                pl.BlockSpec((slots, HD, wide), lambda i, a, b: (0, head + a[slots], 0)),
            ]
            + [whole(part.shape) for part in flat],
            out_specs=tuple(whole(shape.shape) for shape in shapes),
            scratch_shapes=[
                pltpu.VMEM((blocks * rows, HD), jnp.bfloat16),
                pltpu.VMEM((HD + STAT_ROWS, blocks * rows), jnp.bfloat16),
                pltpu.VMEM((2, blocks * rows, wide), jnp.float32),
                pltpu.VMEM((2, 8, wide), jnp.float32),
                pltpu.VMEM((slots, HD, wide), jnp.float32),
                pltpu.VMEM((slots, 8, wide), jnp.float32),
            ],
        ),
        compiler_params=pltpu.CompilerParams(vmem_limit_bytes=2 * SMALL),
        cost_estimate=pl.CostEstimate(
            flops=8 * per * blocks * rows * wide * HD,
            bytes_accessed=blocks * rows * HD * 16 + slots * HD * wide * 4,
            transcendentals=per * blocks * rows * wide,
        ),
        name="attend",
    )(order, place, *own, cosine, sine, q_all, *flat)


def gather_kernel(parts, keep_ref, keep_log_ref, *rest):
    received = rest[:parts]
    context_ref, log_ref = rest[parts : parts + 2]
    sends = rest[parts + 2 :]
    for slot in range(keep_ref.shape[0]):
        pieces = [(keep_ref[slot], keep_log_ref[slot][:1])] + [unpack(part[slot]) for part in received]
        context, logsum = blend(pieces)
        if slot == 0:
            context_ref[...] = context
            log_ref[...] = jnp.broadcast_to(logsum, log_ref.shape)
        else:
            packed, stats = pack(context, logsum)
            sends[slot - 1][:HD] = packed
            sends[slot - 1][HD:] = stats


def gather(keep, keep_log, received):
    count, _, wide = keep.shape
    shapes = [
        jax.ShapeDtypeStruct((HD, wide), jnp.float32),
        jax.ShapeDtypeStruct((8, wide), jnp.float32),
    ] + [jax.ShapeDtypeStruct((HD + STAT_ROWS, wide), jnp.bfloat16)] * (count - 1)
    outs = pl.pallas_call(
        functools.partial(gather_kernel, len(received)),
        out_shape=tuple(shapes),
        compiler_params=pltpu.CompilerParams(vmem_limit_bytes=SMALL),
        cost_estimate=pl.CostEstimate(
            flops=4 * (len(received) + 1) * count * HD * wide,
            bytes_accessed=count * HD * wide * (6 + 2 * len(received)),
            transcendentals=0,
        ),
        name="gather",
    )(keep, keep_log, *received)
    return outs[0], outs[1], list(outs[2:])


def finish_kernel(split, aliased, core_ref, context_ref, log_ref, *rest):
    received = rest[: 2 * split - 1]
    cache_ref, cache_log_ref = rest[2 * split - 1 : 2 * split + 1]
    out_ref = rest[2 * split + 1 + aliased]
    core = core_ref[0]
    rows, heads = out_ref.shape[:2]
    done = []
    for apart in range(split):
        pieces = []
        if apart == 0:
            pieces.append((context_ref[...], log_ref[:1]))
        else:
            pieces.append(unpack(received[apart - 1][...]))
        pieces.append(unpack(received[split - 1 + apart][...]))
        pieces.append((cache_ref[core ^ apart], cache_log_ref[core ^ apart][:1]))
        context, _ = blend(pieces)
        done.append(jnp.transpose(context).reshape(rows, heads // split, HD))
    if split == 2:
        first = jnp.where(core == 0, done[0], done[1])
        second = jnp.where(core == 0, done[1], done[0])
        done = [jnp.concatenate([first, second], 1)]
    out_ref[...] = done[0].astype(out_ref.dtype)


def finish(core, context, log, received, cache, cache_log, split, chunk, shape, before):
    wide = context.shape[1]
    rows, all_heads, _ = shape
    part = all_heads * split // cache.shape[0]

    def whole(array):
        return pl.BlockSpec(array.shape, lambda i, c: (0,) * array.ndim)

    operands = [context, log, *received]
    specs = [whole(array) for array in operands]
    operands += [cache, cache_log]
    specs += [
        pl.BlockSpec((split, HD, wide), lambda i, c: (chunk, 0, 0)),
        pl.BlockSpec((split, 8, wide), lambda i, c: (chunk, 0, 0)),
    ]
    aliases = {}
    if before is not None:
        operands.append(before)
        specs.append(ANY)
        aliases = {len(operands): 0}
    return pl.pallas_call(
        functools.partial(finish_kernel, split, before is not None),
        out_shape=jax.ShapeDtypeStruct(shape, jnp.bfloat16),
        grid_spec=pltpu.PrefetchScalarGridSpec(
            num_scalar_prefetch=1,
            grid=(1,),
            in_specs=specs,
            out_specs=pl.BlockSpec((rows, part, HD), lambda i, c: (0, chunk, 0)),
        ),
        input_output_aliases=aliases,
        compiler_params=pltpu.CompilerParams(vmem_limit_bytes=SMALL),
        cost_estimate=pl.CostEstimate(
            flops=8 * split * HD * wide, bytes_accessed=16 * split * HD * wide, transcendentals=0
        ),
        name="finish",
    )(core.reshape(1), *operands)


def tables(starts, rows):
    half_width = HD // 2
    inverse_freq = 500000.0 ** (-(jnp.arange(half_width, dtype=jnp.float32) * 2.0 / HD))
    lane = jnp.arange(HD, dtype=jnp.int32)[None, :]
    start = jnp.where(lane < half_width, starts[0], starts[1])
    positions = start + jnp.arange(rows, dtype=jnp.int32)[:, None]
    angles = positions.astype(jnp.float32) * jnp.concatenate([inverse_freq, inverse_freq])[None, :]
    return jnp.cos(angles), jnp.sin(angles)


def on_device(
    prefill_states,
    key_weight,
    value_weight,
    offsets,
    matching,
    queries,
    cache_keys,
    cache_values,
    cache_lengths,
):
    tp = lax.axis_size("tp")
    groups = lax.axis_size("grp")
    me = lax.axis_index("grp").astype(jnp.int32)
    rank = lax.axis_index("tp").astype(jnp.int32)
    block_len = prefill_states.shape[0]
    kv_local = key_weight.shape[1] // HD // tp
    row_count = queries.shape[0]
    group_size = queries.shape[1] // kv_local
    wide = row_count * group_size
    split = 2 if kv_local % 2 == 0 else 1
    chunks = kv_local // split
    per = groups // PROMPTS
    homes = per // split
    keep = PROMPTS * split
    core = me % split
    spot = (me // split) % homes
    side = me // per

    grouped = queries.reshape(row_count, kv_local, group_size, HD)
    turned = grouped.transpose(1, 3, 0, 2).reshape(kv_local * HD, wide)
    tag = jnp.broadcast_to(matching[0].astype(jnp.bfloat16), (STAT_ROWS, wide))
    q_all = lax.all_gather(jnp.concatenate([turned, tag], 0), "grp")
    wanted = q_all[:, kv_local * HD, 0].astype(jnp.int32)
    starts = [offsets] + [
        lax.ppermute(offsets, "grp", [(i, i ^ apart) for i in range(groups)]) for apart in range(1, split)
    ]

    def exchange(array, shift, apart):
        pairs = [
            (g * tp + t, (g ^ apart) * tp + (t + shift) % tp) for g in range(groups) for t in range(tp)
        ]
        return lax.ppermute(array, ("grp", "tp"), pairs)

    received = [[[] for _ in range(split)] for _ in range(chunks)]
    own = [None] * chunks

    def column(shift, chunk):
        return ((rank + shift) % tp) * chunks + chunk

    def run(jobs, core):
        results = project(
            prefill_states,
            key_weight,
            value_weight,
            core,
            [column(shift, chunk) for shift, chunk in jobs],
            ["own" if shift == 0 else "send" for shift, _ in jobs],
            split,
        )
        results, core = lax.optimization_barrier((results, core))
        for (shift, chunk), outs in zip(jobs, results):
            if shift == 0:
                own[chunk] = outs[:2]
                outs = [None] + outs[2:]
            for apart in range(split):
                if outs[apart] is not None:
                    received[chunk][apart].append(exchange(outs[apart], shift, apart))
        return core

    jobs = [(shift, chunk) for chunk in range(chunks) for shift in range(1, tp)]
    later = run(jobs[:1], core)
    run(jobs[1:] + [(0, chunk) for chunk in range(chunks)], later)

    cosine, sine = tables((starts[0][0], starts[-1][0]), block_len)
    mine = (wanted == side).astype(jnp.int32)
    before = jnp.cumsum(mine)
    names = jnp.arange(groups, dtype=jnp.int32)
    target = jnp.where(mine == 1, before - 1, per + names - before)
    order = jnp.sum(jnp.where(target[None, :] == names[:, None], names[None, :], 0), 1).astype(jnp.int32)
    away = ((order // split) % homes) ^ spot
    place = (away * PROMPTS + ((order // per) ^ side)) * split + (order % split ^ core)
    order = jnp.concatenate([order, core.reshape(1)])

    grouped, own[-1] = lax.optimization_barrier((grouped, own[-1]))
    score_scale = HD ** (-0.5)
    cache_len = cache_keys.shape[2]
    cache_scores = (
        jnp.einsum("rkgd,rktd->rkgt", grouped, cache_keys, preferred_element_type=jnp.float32)
        * score_scale
    )
    alive = (jnp.arange(cache_len, dtype=jnp.int32)[None, :] < cache_lengths[:, None])[:, None, None, :]
    cache_scores = jnp.where(alive, cache_scores, EMPTY)
    cache_top = cache_scores.max(-1)
    cache_weights = jnp.where(alive, jnp.exp(cache_scores - cache_top[..., None]), 0.0)
    cache_total = cache_weights.sum(-1)
    cache_sum = jnp.einsum(
        "rkgt,rktd->rkgd",
        cache_weights.astype(jnp.bfloat16),
        cache_values,
        preferred_element_type=jnp.float32,
    )
    cache_context = cache_sum / cache_total[..., None]
    cache_context = cache_context.transpose(1, 3, 0, 2).reshape(kv_local, HD, wide)
    cache_log = cache_top * LOG2E + jnp.log2(cache_total)
    cache_log = cache_log.transpose(1, 0, 2).reshape(kv_local, 1, wide)
    cache_log = jnp.broadcast_to(cache_log, (kv_local, 8, wide))
    cache_context, cache_log, order, place = lax.optimization_barrier((cache_context, cache_log, order, place))

    def partner(i, side_apart, apart):
        return (i + side_apart * per) % groups ^ apart

    result = None
    for chunk in range(chunks):
        outs = attend(order, place, own[chunk], cosine, sine, q_all, received[chunk], chunk * split, per, keep)
        outs, order = lax.optimization_barrier((outs, order))
        arrived = [
            lax.ppermute(outs[2 + far - 1], "grp", [(i, i ^ (far * split)) for i in range(groups)])
            for far in range(1, homes)
        ]
        context, log, sends = gather(outs[0], outs[1], arrived)
        final = [
            lax.ppermute(
                sends[number - 1],
                "grp",
                [(i, partner(i, number // split, number % split)) for i in range(groups)],
            )
            for number in range(1, keep)
        ]
        result = finish(
            core, context, log, final, cache_context, cache_log, split, chunk, queries.shape, result
        )
    return result


def solution(mesh):
    placed = (
        P("grp", "tp"),
        P("tp", None),
        P("tp", None),
        P("grp"),
        P("grp"),
        P("grp", "tp", None),
        P("grp", "tp", None, None),
        P("grp", "tp", None, None),
        P("grp"),
    )
    return jax.shard_map(
        on_device, mesh=mesh, in_specs=placed, out_specs=P("grp", "tp", None), check_vma=False
    )
```

```python
import functools

import jax
import jax.numpy as jnp
from jax import lax
from jax.experimental import pallas as pl
from jax.experimental.pallas import tpu as pltpu
from jax.sharding import PartitionSpec as P

HD = 128
PROMPTS = 2
CODE_BLOCKS = 16
CODE_TOP = 32000.0
STAT_ROWS = 16
EMPTY = -1e30
LOG2E = 1.4426950408889634
TO_LOG2 = HD ** (-0.5) * LOG2E
BIG = 60 * 1024 * 1024
SMALL = 16 * 1024 * 1024
ANY = pl.BlockSpec(memory_space=pl.ANY)


def encode(values):
    rows = values.shape[0]
    blocks = values.reshape(CODE_BLOCKS, rows // CODE_BLOCKS, HD)
    largest = jnp.maximum(jnp.max(jnp.abs(blocks), axis=1), 1e-30)
    exponent = jnp.floor(jnp.log(largest) * LOG2E) + 1.0
    factor = jnp.exp2(-exponent) * CODE_TOP
    codes = (blocks * factor[:, None, :]).astype(jnp.int32).astype(jnp.int16)
    return codes.reshape(rows, HD), exponent.astype(jnp.int32).astype(jnp.int16)


def decode(codes, exponent):
    rows = codes.shape[0]
    factor = jnp.exp2(exponent.astype(jnp.int32).astype(jnp.float32)) * (1.0 / CODE_TOP)
    blocks = codes.astype(jnp.int32).astype(jnp.float32).reshape(CODE_BLOCKS, rows // CODE_BLOCKS, HD)
    return (blocks * factor[:, None, :]).reshape(rows, HD)


def project_kernel(plan, split, pieces, place_ref, x_hbm, wk_hbm, wv_hbm, *rest):
    count = sum(split - (kind == "own") for kind in plan) + 2 * plan.count("own")
    outs = list(rest[:count])
    x_ref, wk_ref, wv_ref, acc, x_sems, wk_sems, wv_sems = rest[count:]
    rows, depth = x_ref.shape
    width = wk_ref.shape[2]
    part = depth // pieces
    core = place_ref[0]

    def x_copy(piece):
        window = pl.ds(pl.multiple_of(piece * part, part), part)
        return pltpu.make_async_copy(x_hbm.at[:, window], x_ref.at[:, window], x_sems.at[piece])

    def weight_copies(step, piece):
        window = pl.ds(pl.multiple_of(piece * part, part), part)
        lanes = pl.ds(pl.multiple_of(place_ref[1 + step] * width, width), width)
        return [
            pltpu.make_async_copy(hbm.at[window, lanes], ref.at[step % 2, window], sems.at[step % 2, piece])
            for hbm, ref, sems in ((wk_hbm, wk_ref, wk_sems), (wv_hbm, wv_ref, wv_sems))
        ]

    for piece in range(pieces):
        x_copy(piece).start()
        for copy in weight_copies(0, piece):
            copy.start()
    for step, kind in enumerate(plan):
        if step + 1 < len(plan):
            for piece in range(pieces):
                for copy in weight_copies(step + 1, piece):
                    copy.start()

        for piece in range(pieces):
            if step == 0:
                x_copy(piece).wait()
            for copy in weight_copies(step, piece):
                copy.wait()
            window = slice(piece * part, (piece + 1) * part)
            left = x_ref[:, window]
            for half, ref in ((0, wk_ref), (1, wv_ref)):
                lanes = slice(half * width, (half + 1) * width)
                term = jnp.dot(left, ref[step % 2, window], preferred_element_type=jnp.float32)
                if piece == 0:
                    acc[:, lanes] = term
                else:
                    acc[:, lanes] += term
        for apart in range(split):
            lanes = pl.multiple_of((core ^ apart) * HD, HD)
            if kind == "own" and apart == 0:
                outs.pop(0)[...] = acc[:, pl.ds(lanes, HD)]
                outs.pop(0)[...] = acc[:, pl.ds(width + lanes, HD)]
                continue
            ref = outs.pop(0)
            for half in range(2):
                codes, exponent = encode(acc[:, pl.ds(half * width + lanes, HD)])
                ref[:rows, half * HD : (half + 1) * HD] = codes
                ref[rows:, half * HD : (half + 1) * HD] = exponent


def project(x, wk, wv, core, columns, plan, split):
    rows, depth = x.shape
    width = split * HD
    steps = len(plan)
    pieces = 4
    coded = jax.ShapeDtypeStruct((rows + CODE_BLOCKS, 2 * HD), jnp.int16)
    plain = jax.ShapeDtypeStruct((rows, HD), jnp.float32)
    shapes = []
    for kind in plan:
        shapes += ([plain, plain] if kind == "own" else [coded]) + [coded] * (split - 1)
    place = jnp.stack([core] + columns).astype(jnp.int32)
    outs = pl.pallas_call(
        functools.partial(project_kernel, plan, split, pieces),
        out_shape=tuple(shapes),
        grid_spec=pltpu.PrefetchScalarGridSpec(
            num_scalar_prefetch=1,
            grid=(1,),
            in_specs=[ANY, ANY, ANY],
            out_specs=tuple(pl.BlockSpec(shape.shape, lambda s, p: (0, 0)) for shape in shapes),
            scratch_shapes=[
                pltpu.VMEM((rows, depth), x.dtype),
                pltpu.VMEM((2, depth, width), wk.dtype),
                pltpu.VMEM((2, depth, width), wv.dtype),
                pltpu.VMEM((rows, 2 * width), jnp.float32),
                pltpu.SemaphoreType.DMA((pieces,)),
                pltpu.SemaphoreType.DMA((2, pieces)),
                pltpu.SemaphoreType.DMA((2, pieces)),
            ],
        ),
        compiler_params=pltpu.CompilerParams(vmem_limit_bytes=BIG),
        cost_estimate=pl.CostEstimate(
            flops=rows * depth, bytes_accessed=rows * depth // 4, transcendentals=0
        ),
        name="project",
    )(place, x, wk, wv)
    results = []
    index = 0
    for kind in plan:
        size = split + (kind == "own")
        results.append(list(outs[index : index + size]))
        index += size
    return results


def pack(context, logsum):
    high = logsum.astype(jnp.bfloat16).astype(jnp.float32)
    middle = (logsum - high).astype(jnp.bfloat16).astype(jnp.float32)
    low = logsum - high - middle
    line = lax.broadcasted_iota(jnp.int32, (STAT_ROWS, context.shape[1]), 0)
    stats = jnp.where(line == 0, high, jnp.where(line == 1, middle, jnp.where(line == 2, low, 0.0)))
    return context.astype(jnp.bfloat16), stats.astype(jnp.bfloat16)


def unpack(block):
    stats = block[HD:].astype(jnp.float32)
    return block[:HD].astype(jnp.float32), stats[0:1] + stats[1:2] + stats[2:3]


def blend(pieces):
    top = functools.reduce(jnp.maximum, [logsum for _, logsum in pieces])
    shares = [jnp.exp2(logsum - top) for _, logsum in pieces]
    total = functools.reduce(jnp.add, shares)
    inverse = 1.0 / total
    context = functools.reduce(
        jnp.add, [context * (share * inverse) for (context, _), share in zip(pieces, shares)]
    )
    return context, top + jnp.log(total) * LOG2E


def attend_kernel(layout, per, slots, keep, sends, order_ref, place_ref, own_key, own_value, cos_ref, sin_ref, q_ref, *rest):
    parts = sum(layout)
    received = list(rest[:parts])
    keep_ref, keep_log_ref = rest[parts : parts + 2]
    send_refs = rest[parts + 2 : parts + 2 + sends]
    key_scr, value_scr, score_scr, top_scr, context_scr, log_scr = rest[parts + 2 + sends :]
    rows = own_key.shape[0]
    blocks = len(layout)
    for block in range(blocks):
        here = [received.pop(0) for _ in range(layout[block])]
        for is_value in range(2):
            lanes = slice(is_value * HD, (is_value + 1) * HD)
            terms = [decode(part[:rows, lanes], part[rows:, lanes]) for part in here]
            if block == 0:
                terms = [(own_value if is_value else own_key)[...]] + terms
            whole = functools.reduce(jnp.add, terms)
            window = slice(block * rows, (block + 1) * rows)
            if is_value:
                value_scr[:HD, window] = jnp.transpose(whole).astype(jnp.bfloat16)
            else:
                cosine = cos_ref[...]
                sine = sin_ref[...]
                low = lax.broadcasted_iota(jnp.int32, cosine.shape, 1) < HD // 2
                mine = low if block == 0 else ~low
                cosine = jnp.where(mine, cosine, pltpu.roll(cosine, HD // 2, 1))
                sine = jnp.where(mine, sine, pltpu.roll(sine, HD // 2, 1))
                sine = jnp.where(low, -sine, sine)
                whole = whole * cosine + pltpu.roll(whole, HD // 2, 1) * sine
                key_scr[window] = whole.astype(jnp.bfloat16)
    value_scr[HD:] = jnp.ones((STAT_ROWS, blocks * rows), jnp.bfloat16)
    total_keys = blocks * rows
    tile = min(512, total_keys)

    def score(index, buffer):
        query = q_ref[order_ref[index]]
        tops = []
        for start in range(0, total_keys, tile):
            scores = jnp.dot(key_scr[start : start + tile], query, preferred_element_type=jnp.float32)
            score_scr[buffer, start : start + tile] = scores
            tops.append(jnp.max(scores, axis=0, keepdims=True))
        top = functools.reduce(jnp.maximum, tops) * TO_LOG2
        top_scr[buffer] = jnp.broadcast_to(top, top_scr.shape[1:])

    def weigh(index, buffer):
        top = top_scr[buffer][:1]
        summed = None
        for start in range(0, total_keys, tile):
            weights = jnp.exp2(score_scr[buffer, start : start + tile] * TO_LOG2 - top).astype(jnp.bfloat16)
            term = jnp.dot(value_scr[:, start : start + tile], weights, preferred_element_type=jnp.float32)
            summed = term if summed is None else summed + term
        total = summed[HD : HD + 1]
        context_scr[place_ref[index]] = summed[:HD] * (1.0 / total)
        log_scr[place_ref[index]] = jnp.broadcast_to(top + jnp.log(total) * LOG2E, log_scr.shape[1:])

    score(0, 0)

    @pl.loop(0, per // 2)
    def _(pair):
        score(2 * pair + 1, 1)
        weigh(2 * pair, 0)
        score(jnp.minimum(2 * pair + 2, per - 1), 0)
        weigh(2 * pair + 1, 1)

    @pl.loop(per, slots)
    def _(index):
        context_scr[place_ref[index]] = jnp.zeros(context_scr.shape[1:], jnp.float32)
        log_scr[place_ref[index]] = jnp.full(log_scr.shape[1:], EMPTY, jnp.float32)

    for slot in range(keep):
        keep_ref[slot] = context_scr[slot]
        keep_log_ref[slot] = log_scr[slot]
    for number, send_ref in enumerate(send_refs):
        for slot in range(keep):
            where = (number + 1) * keep + slot
            context, stats = pack(context_scr[where], log_scr[where][:1])
            send_ref[slot, :HD] = context
            send_ref[slot, HD:] = stats


def attend(order, place, own, cosine, sine, q_all, received, per, keep):
    rows = own[0].shape[0]
    slots, _, wide = q_all.shape
    blocks = len(received)
    layout = [len(parts) for parts in received]
    flat = [part for parts in received for part in parts]
    sends = slots // keep - 1

    def whole(shape):
        return pl.BlockSpec(shape, lambda i, a, b: (0,) * len(shape))

    shapes = [
        jax.ShapeDtypeStruct((keep, HD, wide), jnp.float32),
        jax.ShapeDtypeStruct((keep, 8, wide), jnp.float32),
    ] + [jax.ShapeDtypeStruct((keep, HD + STAT_ROWS, wide), jnp.bfloat16)] * sends
    return pl.pallas_call(
        functools.partial(attend_kernel, layout, per, slots, keep, sends),
        out_shape=tuple(shapes),
        grid_spec=pltpu.PrefetchScalarGridSpec(
            num_scalar_prefetch=2,
            grid=(1,),
            in_specs=[
                whole((rows, HD)),
                whole((rows, HD)),
                whole((rows, HD)),
                whole((rows, HD)),
                pl.BlockSpec((slots, HD, wide), lambda i, a, b: (0, 0, 0)),
            ]
            + [whole(part.shape) for part in flat],
            out_specs=tuple(whole(shape.shape) for shape in shapes),
            scratch_shapes=[
                pltpu.VMEM((blocks * rows, HD), jnp.bfloat16),
                pltpu.VMEM((HD + STAT_ROWS, blocks * rows), jnp.bfloat16),
                pltpu.VMEM((2, blocks * rows, wide), jnp.float32),
                pltpu.VMEM((2, 8, wide), jnp.float32),
                pltpu.VMEM((slots, HD, wide), jnp.float32),
                pltpu.VMEM((slots, 8, wide), jnp.float32),
            ],
        ),
        compiler_params=pltpu.CompilerParams(vmem_limit_bytes=2 * SMALL),
        cost_estimate=pl.CostEstimate(
            flops=rows * HD, bytes_accessed=rows * HD, transcendentals=0
        ),
        name="attend",
    )(order, place, *own, cosine, sine, q_all, *flat)


def gather_kernel(parts, keep_ref, keep_log_ref, *rest):
    received = rest[:parts]
    context_ref, log_ref = rest[parts : parts + 2]
    sends = rest[parts + 2 :]
    for slot in range(keep_ref.shape[0]):
        pieces = [(keep_ref[slot], keep_log_ref[slot][:1])] + [unpack(part[slot]) for part in received]
        context, logsum = blend(pieces)
        if slot == 0:
            context_ref[...] = context
            log_ref[...] = jnp.broadcast_to(logsum, log_ref.shape)
        else:
            packed, stats = pack(context, logsum)
            sends[slot - 1][:HD] = packed
            sends[slot - 1][HD:] = stats


def gather(keep, keep_log, received):
    count, _, wide = keep.shape
    shapes = [
        jax.ShapeDtypeStruct((HD, wide), jnp.float32),
        jax.ShapeDtypeStruct((8, wide), jnp.float32),
    ] + [jax.ShapeDtypeStruct((HD + STAT_ROWS, wide), jnp.bfloat16)] * (count - 1)
    outs = pl.pallas_call(
        functools.partial(gather_kernel, len(received)),
        out_shape=tuple(shapes),
        compiler_params=pltpu.CompilerParams(vmem_limit_bytes=SMALL),
        cost_estimate=pl.CostEstimate(
            flops=4 * (len(received) + 1) * count * HD * wide,
            bytes_accessed=count * HD * wide * (6 + 2 * len(received)),
            transcendentals=0,
        ),
        name="gather",
    )(keep, keep_log, *received)
    return outs[0], outs[1], list(outs[2:])


def finish_kernel(split, aliased, core_ref, context_ref, log_ref, *rest):
    received = rest[: 2 * split - 1]
    cache_ref, cache_log_ref = rest[2 * split - 1 : 2 * split + 1]
    out_ref = rest[2 * split + 1 + aliased]
    core = core_ref[0]
    rows, heads = out_ref.shape[:2]
    done = []
    for apart in range(split):
        pieces = []
        if apart == 0:
            pieces.append((context_ref[...], log_ref[:1]))
        else:
            pieces.append(unpack(received[apart - 1][...]))
        pieces.append(unpack(received[split - 1 + apart][...]))
        pieces.append((cache_ref[core ^ apart], cache_log_ref[core ^ apart][:1]))
        context, _ = blend(pieces)
        done.append(jnp.transpose(context).reshape(rows, heads // split, HD))
    if split == 2:
        first = jnp.where(core == 0, done[0], done[1])
        second = jnp.where(core == 0, done[1], done[0])
        done = [jnp.concatenate([first, second], 1)]
    out_ref[...] = done[0].astype(out_ref.dtype)


def finish(core, context, log, received, cache, cache_log, split, chunk, shape, before):
    wide = context.shape[1]
    rows, all_heads, _ = shape
    part = all_heads * split // cache.shape[0]

    def whole(array):
        return pl.BlockSpec(array.shape, lambda i, c: (0,) * array.ndim)

    operands = [context, log, *received]
    specs = [whole(array) for array in operands]
    operands += [cache, cache_log]
    specs += [
        pl.BlockSpec((split, HD, wide), lambda i, c: (chunk, 0, 0)),
        pl.BlockSpec((split, 8, wide), lambda i, c: (chunk, 0, 0)),
    ]
    aliases = {}
    if before is not None:
        operands.append(before)
        specs.append(ANY)
        aliases = {len(operands): 0}
    return pl.pallas_call(
        functools.partial(finish_kernel, split, before is not None),
        out_shape=jax.ShapeDtypeStruct(shape, jnp.bfloat16),
        grid_spec=pltpu.PrefetchScalarGridSpec(
            num_scalar_prefetch=1,
            grid=(1,),
            in_specs=specs,
            out_specs=pl.BlockSpec((rows, part, HD), lambda i, c: (0, chunk, 0)),
        ),
        input_output_aliases=aliases,
        compiler_params=pltpu.CompilerParams(vmem_limit_bytes=SMALL),
        cost_estimate=pl.CostEstimate(
            flops=8 * split * HD * wide, bytes_accessed=16 * split * HD * wide, transcendentals=0
        ),
        name="finish",
    )(core.reshape(1), *operands)


def tables(starts, rows):
    half_width = HD // 2
    inverse_freq = 500000.0 ** (-(jnp.arange(half_width, dtype=jnp.float32) * 2.0 / HD))
    lane = jnp.arange(HD, dtype=jnp.int32)[None, :]
    start = jnp.where(lane < half_width, starts[0], starts[1])
    positions = start + jnp.arange(rows, dtype=jnp.int32)[:, None]
    angles = positions.astype(jnp.float32) * jnp.concatenate([inverse_freq, inverse_freq])[None, :]
    return jnp.cos(angles), jnp.sin(angles)


def on_device(
    prefill_states,
    key_weight,
    value_weight,
    offsets,
    matching,
    queries,
    cache_keys,
    cache_values,
    cache_lengths,
):
    tp = lax.axis_size("tp")
    groups = lax.axis_size("grp")
    me = lax.axis_index("grp").astype(jnp.int32)
    rank = lax.axis_index("tp").astype(jnp.int32)
    block_len = prefill_states.shape[0]
    kv_local = key_weight.shape[1] // HD // tp
    row_count = queries.shape[0]
    group_size = queries.shape[1] // kv_local
    wide = row_count * group_size
    split = 2 if kv_local % 2 == 0 else 1
    chunks = kv_local // split
    per = groups // PROMPTS
    homes = per // split
    keep = PROMPTS * split
    core = me % split
    spot = (me // split) % homes
    side = me // per

    grouped = queries.reshape(row_count, kv_local, group_size, HD)
    turned = grouped.reshape(row_count, chunks, split, group_size, HD).transpose(2, 1, 4, 0, 3)
    turned = turned.reshape(split, chunks * HD, wide)
    line = jnp.arange(STAT_ROWS, dtype=jnp.int32)[:, None]
    tag = jnp.where(line == 0, matching[0], offsets[0]).astype(jnp.bfloat16)
    tag = jnp.broadcast_to(tag, (split, STAT_ROWS, wide))
    turned = jnp.concatenate([turned[:, :HD], tag, turned[:, HD:]], 1)
    own_queries = [lax.dynamic_index_in_dim(turned, core, 0, False)] + [
        lax.ppermute(
            lax.dynamic_index_in_dim(turned, core ^ apart, 0, False),
            "grp",
            [(i, i ^ apart) for i in range(groups)],
        )
        for apart in range(1, split)
    ]
    first = HD + STAT_ROWS
    cuts = [(0, first)] + [(first + chunk * HD, first + (chunk + 1) * HD) for chunk in range(chunks - 1)]
    pieces = [jnp.stack([each[low:high] for each in own_queries]) for low, high in cuts]
    members = [[chip * split + c for chip in range(groups // split)] for c in range(split)]
    gathered = [
        lax.all_gather(piece, "grp", axis_index_groups=members).reshape(groups, -1, wide)
        for piece in pieces
    ]
    starts = jnp.stack([each[HD + 1, 0] for each in own_queries]).astype(jnp.int32)
    own_queries, core = lax.optimization_barrier((own_queries, core))

    def exchange(array, shift, apart):
        pairs = [
            (g * tp + t, (g ^ apart) * tp + (t + shift) % tp) for g in range(groups) for t in range(tp)
        ]
        return lax.ppermute(array, ("grp", "tp"), pairs)

    received = [[[] for _ in range(split)] for _ in range(chunks)]
    own = [None] * chunks

    def column(shift, chunk):
        return ((rank + shift) % tp) * chunks + chunk

    def run(jobs, core):
        results = project(
            prefill_states,
            key_weight,
            value_weight,
            core,
            [column(shift, chunk) for shift, chunk in jobs],
            ["own" if shift == 0 else "send" for shift, _ in jobs],
            split,
        )
        _, core = lax.optimization_barrier((results, core))
        for (shift, chunk), outs in zip(jobs, results):
            if shift == 0:
                own[chunk] = outs[:2]
                outs = [None] + outs[2:]
            for apart in range(split):
                if outs[apart] is not None:
                    received[chunk][apart].append(exchange(outs[apart], shift, apart))
        return core

    jobs = [(shift, chunk) for chunk in range(chunks) for shift in range(1, tp)]
    later = run(jobs[:1], core)
    run(jobs[1:] + [(0, chunk) for chunk in range(chunks)], later)

    gathered[0], received[0] = lax.optimization_barrier((gathered[0], received[0]))
    wanted = gathered[0][:, HD, 0].astype(jnp.int32)
    cosine, sine = tables((starts[0], starts[-1]), block_len)
    mine = (wanted == side).astype(jnp.int32)
    before = jnp.cumsum(mine)
    names = jnp.arange(groups, dtype=jnp.int32)
    target = jnp.where(mine == 1, before - 1, per + names - before)
    order = jnp.sum(jnp.where(target[None, :] == names[:, None], names[None, :], 0), 1).astype(jnp.int32)
    away = ((order // split) % homes) ^ spot
    place = (away * PROMPTS + ((order // per) ^ side)) * split + order % split

    def partner(i, side_apart, apart):
        return (i + side_apart * per) % groups ^ apart

    returned = []
    for chunk in range(chunks):
        outs = attend(
            order, place, own[chunk], cosine, sine, gathered[chunk], received[chunk], per, keep
        )
        outs, order, grouped = lax.optimization_barrier((outs, order, grouped))
        arrived = [
            lax.ppermute(outs[2 + far - 1], "grp", [(i, i ^ (far * split)) for i in range(groups)])
            for far in range(1, homes)
        ]
        returned.append((outs[0], outs[1], arrived))

    score_scale = HD ** (-0.5)
    cache_len = cache_keys.shape[2]
    cache_scores = (
        jnp.einsum("rkgd,rktd->rkgt", grouped, cache_keys, preferred_element_type=jnp.float32)
        * score_scale
    )
    alive = (jnp.arange(cache_len, dtype=jnp.int32)[None, :] < cache_lengths[:, None])[:, None, None, :]
    cache_scores = jnp.where(alive, cache_scores, EMPTY)
    cache_top = cache_scores.max(-1)
    cache_weights = jnp.where(alive, jnp.exp(cache_scores - cache_top[..., None]), 0.0)
    cache_total = cache_weights.sum(-1)
    cache_sum = jnp.einsum(
        "rkgt,rktd->rkgd",
        cache_weights.astype(jnp.bfloat16),
        cache_values,
        preferred_element_type=jnp.float32,
    )
    cache_context = cache_sum / cache_total[..., None]
    cache_context = cache_context.transpose(1, 3, 0, 2).reshape(kv_local, HD, wide)
    cache_log = cache_top * LOG2E + jnp.log2(cache_total)
    cache_log = cache_log.transpose(1, 0, 2).reshape(kv_local, 1, wide)
    cache_log = jnp.broadcast_to(cache_log, (kv_local, 8, wide))
    result = None
    for chunk in range(chunks):
        context, log, sends = gather(*returned[chunk])
        final = [
            lax.ppermute(
                sends[number - 1],
                "grp",
                [(i, partner(i, number // split, number % split)) for i in range(groups)],
            )
            for number in range(1, keep)
        ]
        result = finish(
            core, context, log, final, cache_context, cache_log, split, chunk, queries.shape, result
        )
    return result


def solution(mesh):
    placed = (
        P("grp", "tp"),
        P("tp", None),
        P("tp", None),
        P("grp"),
        P("grp"),
        P("grp", "tp", None),
        P("grp", "tp", None, None),
        P("grp", "tp", None, None),
        P("grp"),
    )
    return jax.shard_map(
        on_device, mesh=mesh, in_specs=placed, out_specs=P("grp", "tp", None), check_vma=False
    )
```

```python
import functools

import jax
import jax.numpy as jnp
from jax import lax
from jax.experimental import pallas as pl
from jax.experimental.pallas import tpu as pltpu
from jax.sharding import PartitionSpec as P

HD = 128
PROMPTS = 2
CODE_BLOCKS = 16
CODE_TOP = 32000.0
STAT_ROWS = 16
EMPTY = -1e30
LOG2E = 1.4426950408889634
TO_LOG2 = HD ** (-0.5) * LOG2E
BIG = 60 * 1024 * 1024
SMALL = 16 * 1024 * 1024
ANY = pl.BlockSpec(memory_space=pl.ANY)
HBM = pl.BlockSpec(memory_space=pltpu.HBM)


def encode(values):
    rows = values.shape[0]
    blocks = values.reshape(CODE_BLOCKS, rows // CODE_BLOCKS, HD)
    largest = jnp.maximum(jnp.max(jnp.abs(blocks), axis=1), 1e-30)
    exponent = jnp.floor(jnp.log(largest) * LOG2E) + 1.0
    factor = jnp.exp2(-exponent) * CODE_TOP
    codes = (blocks * factor[:, None, :]).astype(jnp.int32).astype(jnp.int16)
    return codes.reshape(rows, HD), exponent.astype(jnp.int32).astype(jnp.int16)


def decode(codes, exponent):
    rows = codes.shape[0]
    factor = jnp.exp2(exponent.astype(jnp.int32).astype(jnp.float32)) * (1.0 / CODE_TOP)
    blocks = codes.astype(jnp.int32).astype(jnp.float32).reshape(CODE_BLOCKS, rows // CODE_BLOCKS, HD)
    return (blocks * factor[:, None, :]).reshape(rows, HD)


def project_kernel(plan, split, pieces, place_ref, x_hbm, wk_hbm, wv_hbm, *rest):
    count = sum(split - (kind == "own") for kind in plan) + 2 * plan.count("own")
    outs = list(rest[:count])
    x_ref, wk_ref, wv_ref, acc, x_sems, wk_sems, wv_sems = rest[count:]
    rows, depth = x_ref.shape
    width = wk_ref.shape[2]
    part = depth // pieces
    core = place_ref[0]

    def x_copy(piece):
        window = pl.ds(pl.multiple_of(piece * part, part), part)
        return pltpu.make_async_copy(x_hbm.at[:, window], x_ref.at[:, window], x_sems.at[piece])

    def weight_copies(step, piece):
        window = pl.ds(pl.multiple_of(piece * part, part), part)
        lanes = pl.ds(pl.multiple_of(place_ref[1 + step] * width, width), width)
        return [
            pltpu.make_async_copy(hbm.at[window, lanes], ref.at[step % 2, window], sems.at[step % 2, piece])
            for hbm, ref, sems in ((wk_hbm, wk_ref, wk_sems), (wv_hbm, wv_ref, wv_sems))
        ]

    for piece in range(pieces):
        x_copy(piece).start()
        for copy in weight_copies(0, piece):
            copy.start()
    for step, kind in enumerate(plan):
        if step + 1 < len(plan):
            for piece in range(pieces):
                for copy in weight_copies(step + 1, piece):
                    copy.start()

        for piece in range(pieces):
            if step == 0:
                x_copy(piece).wait()
            for copy in weight_copies(step, piece):
                copy.wait()
            window = slice(piece * part, (piece + 1) * part)
            left = x_ref[:, window]
            for half, ref in ((0, wk_ref), (1, wv_ref)):
                lanes = slice(half * width, (half + 1) * width)
                term = jnp.dot(left, ref[step % 2, window], preferred_element_type=jnp.float32)
                if piece == 0:
                    acc[:, lanes] = term
                else:
                    acc[:, lanes] += term
        for apart in range(split):
            lanes = pl.multiple_of((core ^ apart) * HD, HD)
            if kind == "own" and apart == 0:
                outs.pop(0)[...] = acc[:, pl.ds(lanes, HD)]
                outs.pop(0)[...] = acc[:, pl.ds(width + lanes, HD)]
                continue
            ref = outs.pop(0)
            for half in range(2):
                codes, exponent = encode(acc[:, pl.ds(half * width + lanes, HD)])
                ref[:rows, half * HD : (half + 1) * HD] = codes
                ref[rows:, half * HD : (half + 1) * HD] = exponent


def project(x, wk, wv, core, columns, plan, split):
    rows, depth = x.shape
    width = split * HD
    steps = len(plan)
    pieces = 4
    coded = jax.ShapeDtypeStruct((rows + CODE_BLOCKS, 2 * HD), jnp.int16)
    plain = jax.ShapeDtypeStruct((rows, HD), jnp.float32)
    shapes = []
    for kind in plan:
        shapes += ([plain, plain] if kind == "own" else [coded]) + [coded] * (split - 1)
    place = jnp.stack([core] + columns).astype(jnp.int32)
    outs = pl.pallas_call(
        functools.partial(project_kernel, plan, split, pieces),
        out_shape=tuple(shapes),
        grid_spec=pltpu.PrefetchScalarGridSpec(
            num_scalar_prefetch=1,
            grid=(1,),
            in_specs=[ANY, ANY, ANY],
            out_specs=tuple(pl.BlockSpec(shape.shape, lambda s, p: (0, 0)) for shape in shapes),
            scratch_shapes=[
                pltpu.VMEM((rows, depth), x.dtype),
                pltpu.VMEM((2, depth, width), wk.dtype),
                pltpu.VMEM((2, depth, width), wv.dtype),
                pltpu.VMEM((rows, 2 * width), jnp.float32),
                pltpu.SemaphoreType.DMA((pieces,)),
                pltpu.SemaphoreType.DMA((2, pieces)),
                pltpu.SemaphoreType.DMA((2, pieces)),
            ],
        ),
        compiler_params=pltpu.CompilerParams(vmem_limit_bytes=BIG),
        cost_estimate=pl.CostEstimate(
            flops=4 * rows * depth * width * steps,
            bytes_accessed=2 * rows * depth + steps * (4 * depth * width + 4 * rows * width),
            transcendentals=0,
        ),
        name="project",
    )(place, x, wk, wv)
    results = []
    index = 0
    for kind in plan:
        size = split + (kind == "own")
        results.append(list(outs[index : index + size]))
        index += size
    return results


def pack(context, logsum):
    high = logsum.astype(jnp.bfloat16).astype(jnp.float32)
    middle = (logsum - high).astype(jnp.bfloat16).astype(jnp.float32)
    low = logsum - high - middle
    line = lax.broadcasted_iota(jnp.int32, (STAT_ROWS, context.shape[1]), 0)
    stats = jnp.where(line == 0, high, jnp.where(line == 1, middle, jnp.where(line == 2, low, 0.0)))
    return context.astype(jnp.bfloat16), stats.astype(jnp.bfloat16)


def unpack(block):
    stats = block[HD:].astype(jnp.float32)
    return block[:HD].astype(jnp.float32), stats[0:1] + stats[1:2] + stats[2:3]


def blend(pieces):
    top = functools.reduce(jnp.maximum, [logsum for _, logsum in pieces])
    shares = [jnp.exp2(logsum - top) for _, logsum in pieces]
    total = functools.reduce(jnp.add, shares)
    inverse = 1.0 / total
    context = functools.reduce(
        jnp.add, [context * (share * inverse) for (context, _), share in zip(pieces, shares)]
    )
    return context, top + jnp.log(total) * LOG2E


def attend_kernel(layout, per, slots, keep, sends, chunk_head, order_ref, place_ref, own_key_hbm, own_value_hbm, cos_ref, sin_ref, q_hbm, *rest):
    parts = sum(layout)
    received = list(rest[:parts])
    keep_ref, keep_log_ref = rest[parts : parts + 2]
    send_refs = rest[parts + 2 : parts + 2 + sends]
    key_scr, value_scr, score_scr, top_scr, context_scr, log_scr, own_key, own_value, q_ref, sems = rest[
        parts + 2 + sends :
    ]
    rows = own_key.shape[0]
    lanes = pl.ds(pl.multiple_of((chunk_head + order_ref[slots]) * HD, HD), HD)
    own_copies = [
        pltpu.make_async_copy(own_key_hbm, own_key, sems.at[per]),
        pltpu.make_async_copy(own_value_hbm, own_value, sems.at[per + 1]),
    ]
    query_copies = [
        pltpu.make_async_copy(q_hbm.at[order_ref[index], lanes], q_ref.at[index], sems.at[index])
        for index in range(per)
    ]
    for copy in own_copies + query_copies:
        copy.start()
    for copy in own_copies:
        copy.wait()
    blocks = len(layout)
    for block in range(blocks):
        here = [received.pop(0) for _ in range(layout[block])]
        for is_value in range(2):
            lanes = slice(is_value * HD, (is_value + 1) * HD)
            terms = [decode(part[:rows, lanes], part[rows:, lanes]) for part in here]
            if block == 0:
                terms = [(own_value if is_value else own_key)[...]] + terms
            whole = functools.reduce(jnp.add, terms)
            window = slice(block * rows, (block + 1) * rows)
            if is_value:
                value_scr[:HD, window] = jnp.transpose(whole).astype(jnp.bfloat16)
            else:
                cosine = cos_ref[...]
                sine = sin_ref[...]
                low = lax.broadcasted_iota(jnp.int32, cosine.shape, 1) < HD // 2
                mine = low if block == 0 else ~low
                cosine = jnp.where(mine, cosine, pltpu.roll(cosine, HD // 2, 1))
                sine = jnp.where(mine, sine, pltpu.roll(sine, HD // 2, 1))
                sine = jnp.where(low, -sine, sine)
                whole = whole * cosine + pltpu.roll(whole, HD // 2, 1) * sine
                key_scr[window] = whole.astype(jnp.bfloat16)
    value_scr[HD:] = jnp.ones((STAT_ROWS, blocks * rows), jnp.bfloat16)
    total_keys = blocks * rows
    tile = min(512, total_keys)

    def score(index, buffer):
        query = q_ref[index]
        tops = []
        for start in range(0, total_keys, tile):
            scores = jnp.dot(key_scr[start : start + tile], query, preferred_element_type=jnp.float32)
            score_scr[buffer, start : start + tile] = scores
            tops.append(jnp.max(scores, axis=0, keepdims=True))
        top = functools.reduce(jnp.maximum, tops) * TO_LOG2
        top_scr[buffer] = jnp.broadcast_to(top, top_scr.shape[1:])

    def weigh(index, buffer):
        top = top_scr[buffer][:1]
        summed = None
        for start in range(0, total_keys, tile):
            weights = jnp.exp2(score_scr[buffer, start : start + tile] * TO_LOG2 - top).astype(jnp.bfloat16)
            term = jnp.dot(value_scr[:, start : start + tile], weights, preferred_element_type=jnp.float32)
            summed = term if summed is None else summed + term
        total = summed[HD : HD + 1]
        context_scr[place_ref[index]] = summed[:HD] * (1.0 / total)
        log_scr[place_ref[index]] = jnp.broadcast_to(top + jnp.log(total) * LOG2E, log_scr.shape[1:])

    for copy in query_copies:
        copy.wait()
    score(0, 0)

    @pl.loop(0, per // 2)
    def _(pair):
        score(2 * pair + 1, 1)
        weigh(2 * pair, 0)
        score(jnp.minimum(2 * pair + 2, per - 1), 0)
        weigh(2 * pair + 1, 1)

    @pl.loop(per, slots)
    def _(index):
        context_scr[place_ref[index]] = jnp.zeros(context_scr.shape[1:], jnp.float32)
        log_scr[place_ref[index]] = jnp.full(log_scr.shape[1:], EMPTY, jnp.float32)

    for slot in range(keep):
        keep_ref[slot] = context_scr[slot]
        keep_log_ref[slot] = log_scr[slot]
    for number, send_ref in enumerate(send_refs):
        for slot in range(keep):
            where = (number + 1) * keep + slot
            context, stats = pack(context_scr[where], log_scr[where][:1])
            send_ref[slot, :HD] = context
            send_ref[slot, HD:] = stats


def attend(order, place, own, cosine, sine, q_all, received, head, per, keep):
    rows = own[0].shape[0]
    slots, _, wide = q_all.shape
    blocks = len(received)
    layout = [len(parts) for parts in received]
    flat = [part for parts in received for part in parts]
    sends = slots // keep - 1

    def whole(shape):
        return pl.BlockSpec(shape, lambda i, a, b: (0,) * len(shape))

    shapes = [
        jax.ShapeDtypeStruct((keep, HD, wide), jnp.float32),
        jax.ShapeDtypeStruct((keep, 8, wide), jnp.float32),
    ] + [jax.ShapeDtypeStruct((keep, HD + STAT_ROWS, wide), jnp.bfloat16)] * sends
    return pl.pallas_call(
        functools.partial(attend_kernel, layout, per, slots, keep, sends, head),
        out_shape=tuple(shapes),
        grid_spec=pltpu.PrefetchScalarGridSpec(
            num_scalar_prefetch=2,
            grid=(1,),
            in_specs=[
                HBM,
                HBM,
                whole((rows, HD)),
                whole((rows, HD)),
                HBM,
            ]
            + [whole(part.shape) for part in flat],
            out_specs=tuple(whole(shape.shape) for shape in shapes),
            scratch_shapes=[
                pltpu.VMEM((blocks * rows, HD), jnp.bfloat16),
                pltpu.VMEM((HD + STAT_ROWS, blocks * rows), jnp.bfloat16),
                pltpu.VMEM((2, blocks * rows, wide), jnp.float32),
                pltpu.VMEM((2, 8, wide), jnp.float32),
                pltpu.VMEM((slots, HD, wide), jnp.float32),
                pltpu.VMEM((slots, 8, wide), jnp.float32),
                pltpu.VMEM((rows, HD), jnp.float32),
                pltpu.VMEM((rows, HD), jnp.float32),
                pltpu.VMEM((per, HD, wide), jnp.bfloat16),
                pltpu.SemaphoreType.DMA((per + 2,)),
            ],
        ),
        compiler_params=pltpu.CompilerParams(vmem_limit_bytes=54 * 1024 * 1024),
        cost_estimate=pl.CostEstimate(
            flops=8 * per * blocks * rows * wide * HD,
            bytes_accessed=blocks * rows * HD * 16 + slots * HD * wide * 4,
            transcendentals=per * blocks * rows * wide,
        ),
        name="attend",
    )(order, place, *own, cosine, sine, q_all, *flat)


def gather_kernel(parts, keep_ref, keep_log_ref, *rest):
    received = rest[:parts]
    context_ref, log_ref = rest[parts : parts + 2]
    sends = rest[parts + 2 :]
    for slot in range(keep_ref.shape[0]):
        pieces = [(keep_ref[slot], keep_log_ref[slot][:1])] + [unpack(part[slot]) for part in received]
        context, logsum = blend(pieces)
        if slot == 0:
            context_ref[...] = context
            log_ref[...] = jnp.broadcast_to(logsum, log_ref.shape)
        else:
            packed, stats = pack(context, logsum)
            sends[slot - 1][:HD] = packed
            sends[slot - 1][HD:] = stats


def gather(keep, keep_log, received):
    count, _, wide = keep.shape
    shapes = [
        jax.ShapeDtypeStruct((HD, wide), jnp.float32),
        jax.ShapeDtypeStruct((8, wide), jnp.float32),
    ] + [jax.ShapeDtypeStruct((HD + STAT_ROWS, wide), jnp.bfloat16)] * (count - 1)
    outs = pl.pallas_call(
        functools.partial(gather_kernel, len(received)),
        out_shape=tuple(shapes),
        compiler_params=pltpu.CompilerParams(vmem_limit_bytes=SMALL),
        cost_estimate=pl.CostEstimate(
            flops=4 * (len(received) + 1) * count * HD * wide,
            bytes_accessed=count * HD * wide * (6 + 2 * len(received)),
            transcendentals=0,
        ),
        name="gather",
    )(keep, keep_log, *received)
    return outs[0], outs[1], list(outs[2:])


def finish_kernel(split, aliased, core_ref, context_ref, log_ref, *rest):
    received = rest[: 2 * split - 1]
    cache_ref, cache_log_ref = rest[2 * split - 1 : 2 * split + 1]
    out_ref = rest[2 * split + 1 + aliased]
    core = core_ref[0]
    rows, heads = out_ref.shape[:2]
    done = []
    for apart in range(split):
        pieces = []
        if apart == 0:
            pieces.append((context_ref[...], log_ref[:1]))
        else:
            pieces.append(unpack(received[apart - 1][...]))
        pieces.append(unpack(received[split - 1 + apart][...]))
        pieces.append((cache_ref[core ^ apart], cache_log_ref[core ^ apart][:1]))
        context, _ = blend(pieces)
        done.append(jnp.transpose(context).reshape(rows, heads // split, HD))
    if split == 2:
        first = jnp.where(core == 0, done[0], done[1])
        second = jnp.where(core == 0, done[1], done[0])
        done = [jnp.concatenate([first, second], 1)]
    out_ref[...] = done[0].astype(out_ref.dtype)


def finish(core, context, log, received, cache, cache_log, split, chunk, shape, before):
    wide = context.shape[1]
    rows, all_heads, _ = shape
    part = all_heads * split // cache.shape[0]

    def whole(array):
        return pl.BlockSpec(array.shape, lambda i, c: (0,) * array.ndim)

    operands = [context, log, *received]
    specs = [whole(array) for array in operands]
    operands += [cache, cache_log]
    specs += [
        pl.BlockSpec((split, HD, wide), lambda i, c: (chunk, 0, 0)),
        pl.BlockSpec((split, 8, wide), lambda i, c: (chunk, 0, 0)),
    ]
    aliases = {}
    if before is not None:
        operands.append(before)
        specs.append(ANY)
        aliases = {len(operands): 0}
    return pl.pallas_call(
        functools.partial(finish_kernel, split, before is not None),
        out_shape=jax.ShapeDtypeStruct(shape, jnp.bfloat16),
        grid_spec=pltpu.PrefetchScalarGridSpec(
            num_scalar_prefetch=1,
            grid=(1,),
            in_specs=specs,
            out_specs=pl.BlockSpec((rows, part, HD), lambda i, c: (0, chunk, 0)),
        ),
        input_output_aliases=aliases,
        compiler_params=pltpu.CompilerParams(vmem_limit_bytes=SMALL),
        cost_estimate=pl.CostEstimate(
            flops=8 * split * HD * wide, bytes_accessed=16 * split * HD * wide, transcendentals=0
        ),
        name="finish",
    )(core.reshape(1), *operands)


def tables(starts, rows):
    half_width = HD // 2
    inverse_freq = 500000.0 ** (-(jnp.arange(half_width, dtype=jnp.float32) * 2.0 / HD))
    lane = jnp.arange(HD, dtype=jnp.int32)[None, :]
    start = jnp.where(lane < half_width, starts[0], starts[1])
    positions = start + jnp.arange(rows, dtype=jnp.int32)[:, None]
    angles = positions.astype(jnp.float32) * jnp.concatenate([inverse_freq, inverse_freq])[None, :]
    return jnp.cos(angles), jnp.sin(angles)


def on_device(
    prefill_states,
    key_weight,
    value_weight,
    offsets,
    matching,
    queries,
    cache_keys,
    cache_values,
    cache_lengths,
):
    tp = lax.axis_size("tp")
    groups = lax.axis_size("grp")
    me = lax.axis_index("grp").astype(jnp.int32)
    rank = lax.axis_index("tp").astype(jnp.int32)
    block_len = prefill_states.shape[0]
    kv_local = key_weight.shape[1] // HD // tp
    row_count = queries.shape[0]
    group_size = queries.shape[1] // kv_local
    wide = row_count * group_size
    split = 2 if kv_local % 2 == 0 else 1
    chunks = kv_local // split
    per = groups // PROMPTS
    homes = per // split
    keep = PROMPTS * split
    core = me % split
    spot = (me // split) % homes
    side = me // per

    grouped = queries.reshape(row_count, kv_local, group_size, HD)
    turned = grouped.transpose(1, 3, 0, 2).reshape(kv_local * HD, wide)
    tag = jnp.broadcast_to(matching[0].astype(jnp.bfloat16), (STAT_ROWS, wide))
    q_all = lax.all_gather(jnp.concatenate([turned, tag], 0), "grp")
    wanted = q_all[:, kv_local * HD, 0].astype(jnp.int32)
    starts = [offsets] + [
        lax.ppermute(offsets, "grp", [(i, i ^ apart) for i in range(groups)]) for apart in range(1, split)
    ]

    def exchange(array, shift, apart):
        pairs = [
            (g * tp + t, (g ^ apart) * tp + (t + shift) % tp) for g in range(groups) for t in range(tp)
        ]
        return lax.ppermute(array, ("grp", "tp"), pairs)

    received = [[[] for _ in range(split)] for _ in range(chunks)]
    own = [None] * chunks

    def column(shift, chunk):
        return ((rank + shift) % tp) * chunks + chunk

    def run(jobs, core):
        results = project(
            prefill_states,
            key_weight,
            value_weight,
            core,
            [column(shift, chunk) for shift, chunk in jobs],
            ["own" if shift == 0 else "send" for shift, _ in jobs],
            split,
        )
        results, core = lax.optimization_barrier((results, core))
        for (shift, chunk), outs in zip(jobs, results):
            if shift == 0:
                own[chunk] = outs[:2]
                outs = [None] + outs[2:]
            for apart in range(split):
                if outs[apart] is not None:
                    received[chunk][apart].append(exchange(outs[apart], shift, apart))
        return core

    jobs = [(shift, chunk) for chunk in range(chunks) for shift in range(1, tp)]
    later = run(jobs[:1], core)
    run(jobs[1:] + [(0, chunk) for chunk in range(chunks)], later)

    cosine, sine = tables((starts[0][0], starts[-1][0]), block_len)
    mine = (wanted == side).astype(jnp.int32)
    before = jnp.cumsum(mine)
    names = jnp.arange(groups, dtype=jnp.int32)
    target = jnp.where(mine == 1, before - 1, per + names - before)
    order = jnp.sum(jnp.where(target[None, :] == names[:, None], names[None, :], 0), 1).astype(jnp.int32)
    away = ((order // split) % homes) ^ spot
    place = (away * PROMPTS + ((order // per) ^ side)) * split + (order % split ^ core)
    order = jnp.concatenate([order, core.reshape(1)])

    grouped, own[-1] = lax.optimization_barrier((grouped, own[-1]))
    score_scale = HD ** (-0.5)
    cache_len = cache_keys.shape[2]
    cache_scores = (
        jnp.einsum("rkgd,rktd->rkgt", grouped, cache_keys, preferred_element_type=jnp.float32)
        * score_scale
    )
    alive = (jnp.arange(cache_len, dtype=jnp.int32)[None, :] < cache_lengths[:, None])[:, None, None, :]
    cache_scores = jnp.where(alive, cache_scores, EMPTY)
    cache_top = cache_scores.max(-1)
    cache_weights = jnp.where(alive, jnp.exp(cache_scores - cache_top[..., None]), 0.0)
    cache_total = cache_weights.sum(-1)
    cache_sum = jnp.einsum(
        "rkgt,rktd->rkgd",
        cache_weights.astype(jnp.bfloat16),
        cache_values,
        preferred_element_type=jnp.float32,
    )
    cache_context = cache_sum / cache_total[..., None]
    cache_context = cache_context.transpose(1, 3, 0, 2).reshape(kv_local, HD, wide)
    cache_log = cache_top * LOG2E + jnp.log2(cache_total)
    cache_log = cache_log.transpose(1, 0, 2).reshape(kv_local, 1, wide)
    cache_log = jnp.broadcast_to(cache_log, (kv_local, 8, wide))
    cache_context, cache_log, order, place = lax.optimization_barrier((cache_context, cache_log, order, place))

    def partner(i, side_apart, apart):
        return (i + side_apart * per) % groups ^ apart

    result = None
    for chunk in range(chunks):
        outs = attend(order, place, own[chunk], cosine, sine, q_all, received[chunk], chunk * split, per, keep)
        outs, order = lax.optimization_barrier((outs, order))
        arrived = [
            lax.ppermute(outs[2 + far - 1], "grp", [(i, i ^ (far * split)) for i in range(groups)])
            for far in range(1, homes)
        ]
        context, log, sends = gather(outs[0], outs[1], arrived)
        final = [
            lax.ppermute(
                sends[number - 1],
                "grp",
                [(i, partner(i, number // split, number % split)) for i in range(groups)],
            )
            for number in range(1, keep)
        ]
        result = finish(
            core, context, log, final, cache_context, cache_log, split, chunk, queries.shape, result
        )
    return result


def solution(mesh):
    placed = (
        P("grp", "tp"),
        P("tp", None),
        P("tp", None),
        P("grp"),
        P("grp"),
        P("grp", "tp", None),
        P("grp", "tp", None, None),
        P("grp", "tp", None, None),
        P("grp"),
    )
    return jax.shard_map(
        on_device, mesh=mesh, in_specs=placed, out_specs=P("grp", "tp", None), check_vma=False
    )
```
